256 devices in a mesh: dp: 4 (over x), context: 16 (over z, core), tensor: 4 (over y).
Axes of the slice: x: 4, y: 4, z: 8, core: 2. Of those that a mesh axis runs over, the one named last changes fastest.
Arguments:
- acceptance_vectors: bfloat16 [8192, 4096], P(('dp', 'context'), 'tensor'), may hold values from -6 to 6
- lookup_vectors: bfloat16 [8192, 4096], P(('dp', 'context'), 'tensor'), may hold values from -6 to 6
- payload_vectors: bfloat16 [8192, 4096], P(('dp', 'context'), 'tensor'), may hold values from -6 to 6
- incontext_adaptation: bfloat16 [8192, 4096], P(('dp', 'context'), 'tensor'), may hold values from 0 to 1
- fading_codes: int32 [4, 2048, 64], P('dp', 'context', 'tensor'), may hold values from 1 to 12288
- stacked_line_pointer: int32 [4, 2048], P('dp', 'context'), may hold values from 0 to 8191, as said below
- article_extents: int32 [4, 4], P('dp'), may hold values from 1 to 1024, 2048 in all within a row
- feature_fading: float32 [4096], P('tensor'), may hold values from 3.90625e-05 to 0.03
- erasure_lookup_scaling: float32 [4096], P('tensor'), may hold values from 0.3 to 3
- lookup_mixture_share: float32 [4096], P('tensor'), may hold values from 0 to 1
- reward_coefficients: float32 [4096], P('tensor'), may hold values from -4 to 4
- cluster_standard_scaling: float32 [4096], P('tensor'), may hold values from 0.1 to 1.9
- cluster_standard_offset: float32 [4096], P('tensor'), may hold values from -3 to 3
- final_projection: bfloat16 [4096, 4096], P('tensor'), may hold values from -0.09375 to 0.09375
Outputs:
- summed: bfloat16 [4, 2048, 4096], P('dp', ('context', 'tensor'))
The draws below stay inside these ranges and needn't reach their ends.
Inputs may be any that keep to these rules, and one draw needn't show every extreme that they name: `stacked_line_pointer`: A permutation of 0 to 8191. Each packed shard is 128 consecutive packed rows; its rows fall into consecutive groups of 2, and group g of every shard holds only positions g * 128 to (g + 1) * 128 - 1 of the sequences laid end to end. `article_extents`: each sequence's 4 lengths sum to 2048.
All inputs are finite; a program needn't handle non-finite values.
Results may differ from the reference program's by a relative error of at most 0.019.
Values may be sent and summed in bfloat16 or wider, within the bound.
A program may use at most 128 MiB of HBM per device.

```python
import math
import jax
import jax.numpy as jnp
import numpy as np
from jax import lax

ATTENTION_NUMBER = 64
ATTENTION_SPAN = 64
EMBEDDING_DIM = 4096
TOK_DEV = 128
SUB = 32
DOCS = 4
SEQUENCE_COUNT = 4
SEQUENCE_LENGTH = 2048
PEERS = 64
PEER_ROWS = 2
ROWS = 8192
N_TENSOR = 4


def slow_heads(key, portion):
    ranking = jax.random.permutation(key, ATTENTION_NUMBER)
    chosen = ranking < max(1, int(ATTENTION_NUMBER * portion))
    return jnp.repeat(chosen, ATTENTION_SPAN)


def channel_rates(key, portion):
    slow_mask = slow_heads(key, portion)
    key = jax.random.fold_in(key, 13)
    key_gentle, key_quick = jax.random.split(key)
    spread = jnp.exp(jax.random.uniform(key_gentle, (EMBEDDING_DIM,), jnp.float32, -0.6931, 0.6931))
    lowest = math.log(0.12 / SEQUENCE_LENGTH)
    highest_log = math.log(0.028)
    quick_rate = jnp.exp(jax.random.uniform(key_quick, (EMBEDDING_DIM,), jnp.float32, lowest, highest_log))
    return jnp.where(slow_mask, 0.165 / SEQUENCE_LENGTH * spread, quick_rate)


def draw_feature_fading(key, part):
    rates = channel_rates(key, 0.5)
    return rates.astype(jnp.float32)


def draw_incontext_adaptation(key, part):
    rates = channel_rates(key, 0.5)
    lasting = rates < 1.5 / SEQUENCE_LENGTH
    key = jax.random.fold_in(key, 14)
    uniform_draw = jax.random.uniform(key, (ROWS, EMBEDDING_DIM), jnp.float32)
    fast_value = 0.1 + 0.8 * uniform_draw
    slow_value = (0.2 + 0.8 * uniform_draw) * ATTENTION_SPAN / SEQUENCE_LENGTH
    return jnp.where(lasting[None, :], slow_value, fast_value).astype(jnp.bfloat16)


def draw_fading_codes(key, part):
    key = jax.random.fold_in(key, 12)
    key_magnitude, key_additional, key_expanded = jax.random.split(key, 3)
    blocks = SEQUENCE_LENGTH // TOK_DEV
    level_pick = jax.random.randint(key_magnitude, (SEQUENCE_COUNT, blocks, 1, ATTENTION_NUMBER), 0, 3)
    levels = jnp.left_shift(jnp.ones_like(level_pick), level_pick)
    levels = jnp.broadcast_to(levels, (SEQUENCE_COUNT, blocks, TOK_DEV, ATTENTION_NUMBER)).reshape(SEQUENCE_COUNT, SEQUENCE_LENGTH, ATTENTION_NUMBER)
    decay_code = levels + jax.random.randint(key_additional, (SEQUENCE_COUNT, SEQUENCE_LENGTH, ATTENTION_NUMBER), 0, levels)
    position_slots = jax.random.randint(key_expanded, (SEQUENCE_COUNT, 2), 0, SEQUENCE_LENGTH)
    marked = jnp.any(jnp.arange(SEQUENCE_LENGTH)[None, :, None] == position_slots[:, None, :], axis=2)
    decay_code = jnp.where(marked[:, :, None], 6 * SEQUENCE_LENGTH, decay_code)
    return decay_code.astype(jnp.int32)


def draw_stacked_line_pointer(key, part):
    key = jax.random.fold_in(key, 11)
    keys_all = jax.random.split(key, PEERS)
    orders = jax.vmap(lambda single: jax.random.permutation(single, TOK_DEV))(keys_all)
    source = orders // PEER_ROWS
    within = orders % PEER_ROWS
    target = jnp.arange(PEERS)[:, None]
    slot_rows = source * TOK_DEV + target * PEER_ROWS + within
    return slot_rows.reshape(SEQUENCE_COUNT, SEQUENCE_LENGTH).astype(jnp.int32)


def shard_levels(rng, dims, shards, low, high):
    loudness, own = 1.0, jax.random.fold_in(rng, 6)
    for dim, parts in shards:
        draws = jnp.exp(jax.random.uniform(jax.random.fold_in(own, dim), (parts,), jnp.float32, low / len(shards), high / len(shards)))
        loudness = loudness * jnp.repeat(draws, dims[dim] // parts).reshape([-1 if axis == dim else 1 for axis in range(len(dims))])
    return loudness


def length_profile(count, total, bound, slope):
    loads = [(1 << 20) // math.isqrt(rank ** slope) + 1 for rank in range(2, count + 1)]
    spare, holding = total - bound - (count - 1), [1] * (count - 1)
    while spare > 0:
        movable = [i for i in range(count - 1) if holding[i] < bound]
        mass, left = sum([loads[i] for i in movable]), spare
        for i in movable:
            extra = min(bound - holding[i], max(1, left * loads[i] // mass), spare)
            holding[i] = holding[i] + extra
            spare = spare - extra
    return np.array([bound] + holding)


def uneven(key, count, total, reach, skew):
    if count == 2:
        one = jax.random.randint(key, (), max(1, total - reach), min(reach, total - 1) + 1)
        return jnp.stack([one, total - one])
    tallies = jnp.asarray(length_profile(count, total, reach, skew), jnp.int32)
    couples = (count - 1) // 2
    donor, receiver = tallies[1:1 + 2 * couples:2], tallies[2:2 + 2 * couples:2]
    margin = jnp.minimum(donor - 1, reach - receiver)
    shifted = jax.random.randint(jax.random.fold_in(key, 1), (couples,), 0, 1 << 20) % (margin + 1)
    tallies = tallies.at[1:1 + 2 * couples:2].set(donor - shifted).at[2:2 + 2 * couples:2].set(receiver + shifted)
    return tallies[jax.random.permutation(jax.random.fold_in(key, 2), count)]


def noise(stream_key, shape, scale, reach, cuts=(), kind=jnp.bfloat16):
    array = scale * jax.random.normal(stream_key, shape, jnp.float32)
    if cuts:
        array = array * shard_levels(stream_key, shape, cuts, -0.22, 0.18)
    return jnp.clip(array, -reach, reach).astype(kind)


def setup_inputs(seed: int = 0) -> dict:
    key_list = jax.random.split(jax.random.key(seed), 15)
    return {
        "acceptance_vectors": noise(key_list[0], (ROWS, EMBEDDING_DIM), 1.0, 6.0, ((0, 64), (1, 4))),
        "lookup_vectors": noise(key_list[1], (ROWS, EMBEDDING_DIM), 1.0, 6.0, ((0, 64), (1, 4))),
        "payload_vectors": noise(key_list[2], (ROWS, EMBEDDING_DIM), 1.0, 6.0, ((0, 64), (1, 4))),
        "incontext_adaptation": draw_incontext_adaptation(jax.random.fold_in(key_list[14], 71), 0),
        "fading_codes": draw_fading_codes(jax.random.fold_in(key_list[14], 71), 0),
        "stacked_line_pointer": draw_stacked_line_pointer(jax.random.fold_in(key_list[14], 71), 0),
        "article_extents": jax.vmap(lambda own: uneven(own, DOCS, SEQUENCE_LENGTH, SEQUENCE_LENGTH // 2, 2))(jax.random.split(key_list[6], SEQUENCE_COUNT)).reshape((SEQUENCE_COUNT, DOCS)).astype(jnp.int32),
        "feature_fading": draw_feature_fading(jax.random.fold_in(key_list[14], 71), 0),
        "erasure_lookup_scaling": jnp.clip(jnp.exp(math.log(3.0) - 2.3025851 * jax.random.uniform(key_list[8], (EMBEDDING_DIM,), jnp.float32) ** shard_levels(key_list[8], (EMBEDDING_DIM,), ((0, 4),), -0.2, 0.2)), 0.3, 3.0),
        "lookup_mixture_share": jnp.clip(1.0 * jax.random.uniform(key_list[9], (EMBEDDING_DIM,), jnp.float32) ** shard_levels(key_list[9], (EMBEDDING_DIM,), ((0, 4),), -0.2, 0.2), 0.0, 1.0),
        "reward_coefficients": noise(key_list[10], (EMBEDDING_DIM,), 1.0, 4.0, ((0, 4),), jnp.float32),
        "cluster_standard_scaling": jnp.clip(1.0 + 0.18 * jax.random.normal(key_list[11], (EMBEDDING_DIM,), jnp.float32), 0.1, 1.9),
        "cluster_standard_offset": noise(key_list[12], (EMBEDDING_DIM,), 0.5, 3.0, ((0, 4),), jnp.float32),
        "final_projection": noise(key_list[13], (EMBEDDING_DIM, EMBEDDING_DIM), EMBEDDING_DIM ** -0.5, 0.09375, ((0, 4),)),
    }


highest = lax.Precision.HIGHEST
decay_cap = 0.606531
unit_eps = 1e-06
group_eps = 0.00064

def document_flags(positions, lengths):
    starts = jnp.cumsum(lengths, dtype=jnp.int32) - lengths
    return jnp.any(positions[:, None] == starts[None, :], axis=1).astype(jnp.int32)

def mix_inputs(key_raw, learn_rate, code_rows, rate_grid, scaling_placement, mix_grid):
    scaled = key_raw * scaling_placement
    key_unit = scaled * lax.rsqrt(lax.optimization_barrier(jnp.sum(scaled * scaled, axis=-1, keepdims=True)) + unit_eps)
    lookup_mixture_applied = key_raw * (1.0 + (learn_rate - 1.0) * mix_grid)
    key_erase = key_unit * learn_rate
    log_decay = -decay_cap * (1.0 - jnp.exp(-rate_grid * code_rows.astype(jnp.float32)[..., None]))
    return (lookup_mixture_applied, key_unit, key_erase, log_decay)

def prepare(acceptance_lines, lookup_mixture_applied, key_unit, key_erase, payload_table, log_decay, doc_flags):
    sub_width = acceptance_lines.shape[1]
    key_erase = key_erase * (1 - doc_flags).astype(jnp.float32)[:, :, None, None]
    cum_in = jnp.cumsum(log_decay, axis=1)
    cum_ex = cum_in - log_decay
    count_in = jnp.cumsum(doc_flags, axis=1, dtype=jnp.int32)
    count_ex = count_in - doc_flags
    position_slots = jnp.arange(sub_width)
    strict = (position_slots[:, None] > position_slots[None, :])[None] & (count_ex[:, :, None] == count_in[:, None, :])
    inclusive = (position_slots[:, None] >= position_slots[None, :])[None] & (count_in[:, :, None] == count_in[:, None, :])
    strict_mask = strict.astype(jnp.float32)[:, None]
    inclusive_mask = inclusive.astype(jnp.float32)[:, None]
    unit_up = key_unit * jnp.exp(cum_ex)
    recept_up = acceptance_lines * jnp.exp(cum_in)
    falling = jnp.exp(-cum_in)
    mixed_down = lookup_mixture_applied * falling
    erase_down = key_erase * falling
    erase_mat = jnp.einsum('bthn,bjhn->bhtj', unit_up, erase_down, precision=highest) * strict_mask
    write_mat = jnp.einsum('bthn,bjhn->bhtj', unit_up, mixed_down, precision=highest) * strict_mask
    read_write = jnp.einsum('bthn,bjhn->bhtj', recept_up, mixed_down, precision=highest) * inclusive_mask
    read_erase = jnp.einsum('bthn,bjhn->bhtj', recept_up, erase_down, precision=highest) * inclusive_mask
    negative = -erase_mat
    inverse = jnp.eye(sub_width, dtype=jnp.float32) + negative
    power_mat = negative
    for level_index in range(sub_width.bit_length() - 2):
        power_mat = jnp.einsum('bhtj,bhjs->bhts', power_mat, power_mat, precision=highest)
        inverse = inverse + jnp.einsum('bhtj,bhjs->bhts', inverse, power_mat, precision=highest)
    unit_start = unit_up * (count_ex == 0).astype(jnp.float32)[:, :, None, None]
    recept_start = recept_up * (count_in == 0).astype(jnp.float32)[:, :, None, None]
    last_cum = cum_in[:, -1:]
    last_count = count_in[:, -1:]
    tail_decay = jnp.exp(last_cum - cum_in) * (count_in == last_count).astype(jnp.float32)[:, :, None, None]
    mixed_tail = lookup_mixture_applied * tail_decay
    erase_tail = key_erase * tail_decay
    keep_end = jnp.exp(cum_in[:, -1]) * (count_in[:, -1] == 0).astype(jnp.float32)[:, None, None]
    written = jnp.einsum('bhtj,bjhv->bthv', write_mat, payload_table, precision=highest)
    solved_write = jnp.einsum('bhtj,bjhv->bthv', inverse, written, precision=highest)
    solved_start = jnp.einsum('bhtj,bjhn->bthn', inverse, unit_start, precision=highest)
    out_local = jnp.einsum('bhtj,bjhv->bthv', read_write, payload_table, precision=highest) - jnp.einsum('bhtj,bjhv->bthv', read_erase, solved_write, precision=highest)
    out_carry = recept_start - jnp.einsum('bhtj,bjhn->bthn', read_erase, solved_start, precision=highest)
    diagonal = keep_end[..., :, None] * jnp.eye(acceptance_lines.shape[3], dtype=jnp.float32)
    sub_trans = diagonal - jnp.einsum('bthm,bthn->bhmn', solved_start, erase_tail, precision=highest)
    sub_state = jnp.einsum('bthv,bthn->bhvn', payload_table, mixed_tail, precision=highest) - jnp.einsum('bthv,bthn->bhvn', solved_write, erase_tail, precision=highest)
    return (sub_trans, sub_state, out_carry, out_local)

def final_answer(emitted_lines, acceptance_lines, lookup_mixture_applied, payload_table, reward_placement, scaling_placement, offset_placement):
    reward_contribution = lax.optimization_barrier(jnp.sum(acceptance_lines * lookup_mixture_applied * reward_placement, axis=-1, keepdims=True)) * payload_table
    entire_lines = emitted_lines + reward_contribution
    center = entire_lines - lax.optimization_barrier(jnp.mean(entire_lines, axis=-1, keepdims=True))
    spread = lax.optimization_barrier(jnp.mean(center * center, axis=-1, keepdims=True))
    standardized_lines = center * lax.rsqrt(spread + group_eps) * scaling_placement + offset_placement
    return standardized_lines.reshape(standardized_lines.shape[0], -1).astype(jnp.bfloat16)

def reference(acceptance_vectors, lookup_vectors, payload_vectors, incontext_adaptation, fading_codes, stacked_line_pointer, article_extents, feature_fading, erasure_lookup_scaling, lookup_mixture_share, reward_coefficients, cluster_standard_scaling, cluster_standard_offset, final_projection):
    rate_grid = feature_fading.reshape(ATTENTION_NUMBER, ATTENTION_SPAN)
    scaling_placement = erasure_lookup_scaling.reshape(ATTENTION_NUMBER, ATTENTION_SPAN)
    mix_grid = lookup_mixture_share.reshape(ATTENTION_NUMBER, ATTENTION_SPAN)
    reward_placement = reward_coefficients.reshape(ATTENTION_NUMBER, ATTENTION_SPAN)
    standard_placement = cluster_standard_scaling.reshape(ATTENTION_NUMBER, ATTENTION_SPAN)
    offset_placement = cluster_standard_offset.reshape(ATTENTION_NUMBER, ATTENTION_SPAN)
    sub_count = SEQUENCE_LENGTH // SUB
    group_width = EMBEDDING_DIM // N_TENSOR

    def one_sequence(pieces):
        slot_rows, lengths, code_rows = pieces

        def rows_of(packed):
            return jnp.take(packed, slot_rows, axis=0).astype(jnp.float32).reshape(SEQUENCE_LENGTH, ATTENTION_NUMBER, ATTENTION_SPAN)
        acceptance_lines = rows_of(acceptance_vectors)
        key_raw = rows_of(lookup_vectors)
        payload_table = rows_of(payload_vectors)
        learn_rate = rows_of(incontext_adaptation)
        doc_flags = document_flags(jnp.arange(SEQUENCE_LENGTH, dtype=jnp.int32), lengths)
        lookup_mixture_applied, key_unit, key_erase, log_decay = mix_inputs(key_raw, learn_rate, code_rows, rate_grid, scaling_placement, mix_grid)

        def blocked(item):
            return item.reshape((sub_count, SUB) + item.shape[1:])

        def advance(carried, block_items):
            sub_trans, sub_state, out_carry, out_local = prepare(block_items[0][None], block_items[1][None], block_items[2][None], block_items[3][None], block_items[4][None], block_items[5][None], block_items[6][None])
            emitted_lines = jnp.einsum('hvm,thm->thv', carried, out_carry[0], precision=highest) + out_local[0]
            carried = jnp.einsum('hvm,hmn->hvn', carried, sub_trans[0], precision=highest) + sub_state[0]
            return (carried, emitted_lines)
        initial = jnp.zeros((ATTENTION_NUMBER, ATTENTION_SPAN, ATTENTION_SPAN), jnp.float32)
        final_state, emitted_lines = lax.scan(advance, initial, (blocked(acceptance_lines), blocked(lookup_mixture_applied), blocked(key_unit), blocked(key_erase), blocked(payload_table), blocked(log_decay), blocked(doc_flags)))
        emitted_lines = emitted_lines.reshape(SEQUENCE_LENGTH, ATTENTION_NUMBER, ATTENTION_SPAN)
        standardized_lines = final_answer(emitted_lines, acceptance_lines, lookup_mixture_applied, payload_table, reward_placement, standard_placement, offset_placement)
        accum = jnp.zeros((SEQUENCE_LENGTH, EMBEDDING_DIM), jnp.float32)
        for group_index in range(N_TENSOR):
            lower = group_index * group_width
            product = jnp.dot(standardized_lines[:, lower:lower + group_width], final_projection[lower:lower + group_width], preferred_element_type=jnp.float32)
            rounded = lax.optimization_barrier(product.astype(jnp.bfloat16))
            accum = accum + rounded.astype(jnp.float32)
        return accum.astype(jnp.bfloat16)
    return lax.map(one_sequence, (stacked_line_pointer, article_extents, fading_codes))
```

```python
import functools

import jax
import jax.numpy as jnp
from jax import lax
from jax.experimental import pallas as pl
from jax.experimental.pallas import tpu as pltpu
from jax.sharding import PartitionSpec as P

MESH = pl.DeviceIdType.MESH
SPAN = 64
CHUNK = 64
GROUP = 8
SMALL = 8
decay_cap = 0.606531
unit_eps = 1e-06
group_eps = 0.00064
f32 = jnp.float32
bf16 = jnp.bfloat16


def nn(a, b):
    return lax.dot_general(
        a.astype(bf16), b.astype(bf16), (((1,), (0,)), ((), ())), preferred_element_type=f32
    )


def nt(a, b):
    return lax.dot_general(
        a.astype(bf16), b.astype(bf16), (((1,), (1,)), ((), ())), preferred_element_type=f32
    )


def tn(a, b):
    return lax.dot_general(
        a.astype(bf16), b.astype(bf16), (((0,), (0,)), ((), ())), preferred_element_type=f32
    )


def exchange(
    n_ctx,
    n_peers,
    per_seq,
    r_ref,
    k_ref,
    v_ref,
    a_ref,
    code_ref,
    ptr_ref,
    rows_ref,
    meta_ref,
    packed,
    notes,
    send_sem,
    recv_sem,
    note_send,
    note_recv,
    own_sem,
):
    dp = lax.axis_index("dp")
    ctx = lax.axis_index("context")
    me = dp * n_ctx + ctx
    tensor = lax.axis_index("tensor")

    def place(index):
        return (index // n_ctx, lax.rem(index, n_ctx), tensor)

    barrier = pltpu.get_barrier_semaphore()

    def greet(step, carry):
        other = lax.rem(me + step, n_peers)
        pl.semaphore_signal(barrier, inc=1, device_id=place(other), device_id_type=MESH)
        return carry

    lax.fori_loop(1, n_peers, greet, 0)

    tokens = r_ref.shape[0]
    n_dp = n_peers // n_ctx
    for pair in range(n_ctx // 2):
        lanes = slice(128 * pair, 128 * pair + 128)
        left, right = slice(0, SPAN), slice(SPAN, 128)
        r, k, v, a = r_ref[:, lanes], k_ref[:, lanes], v_ref[:, lanes], a_ref[:, lanes]
        for half, part in ((0, left), (1, right)):
            rk = jnp.concatenate([r[:, part], k[:, part]], axis=1)
            va = jnp.concatenate([v[:, part], a[:, part]], axis=1)
            for s in range(n_dp):
                slot = s * n_ctx + 2 * pair + half
                packed[slot, :, 0:128] = rk[s * per_seq : (s + 1) * per_seq]
                packed[slot, :, 128:256] = va[s * per_seq : (s + 1) * per_seq]

    eye = (
        lax.broadcasted_iota(jnp.int32, (tokens, tokens), 0)
        == lax.broadcasted_iota(jnp.int32, (tokens, tokens), 1)
    ).astype(f32)
    codes = lax.dot_general(
        code_ref[...].astype(f32),
        eye,
        (((0,), (0,)), ((), ())),
        precision=lax.Precision.HIGHEST,
        preferred_element_type=f32,
    )
    pointers = ptr_ref[...].astype(f32)
    for c in range(n_ctx):
        notes[c, 0:1, :] = pointers
        notes[c, 1:2, :] = codes[c : c + 1, :]
        notes[c, 2:8, :] = jnp.zeros((6, tokens), f32)

    pl.semaphore_wait(barrier, n_peers - 1)

    own_rows = pltpu.make_async_copy(packed.at[me], rows_ref.at[me], own_sem.at[0])
    own_rows.start()
    own_note = pltpu.make_async_copy(notes.at[ctx], meta_ref.at[ctx], own_sem.at[1])
    own_note.start()

    def note_copy(step):
        other = lax.rem(ctx + step, n_ctx)
        return pltpu.make_async_remote_copy(
            src_ref=notes.at[other],
            dst_ref=meta_ref.at[ctx],
            send_sem=note_send,
            recv_sem=note_recv,
            device_id=(dp, other, tensor),
            device_id_type=MESH,
        )

    def rows_copy(step):
        other = lax.rem(me + step, n_peers)
        return pltpu.make_async_remote_copy(
            src_ref=packed.at[other],
            dst_ref=rows_ref.at[me],
            send_sem=send_sem,
            recv_sem=recv_sem,
            device_id=place(other),
            device_id_type=MESH,
        )

    def send_note(step, carry):
        note_copy(step).start()
        return carry

    def send_rows(step, carry):
        rows_copy(step).start()
        return carry

    lax.fori_loop(1, n_ctx, send_note, 0)
    lax.fori_loop(1, n_peers, send_rows, 0)
    own_rows.wait()
    own_note.wait()
    rest_rows = rows_ref.at[pl.ds(0, n_peers - 1)]
    rest_notes = meta_ref.at[pl.ds(0, n_ctx - 1)]
    pltpu.make_async_copy(rest_notes, rest_notes, note_send).wait()
    pltpu.make_async_copy(rest_notes, rest_notes, note_recv).wait()
    pltpu.make_async_copy(rest_rows, rest_rows, send_sem).wait()
    pltpu.make_async_copy(rest_rows, rest_rows, recv_sem).wait()


def recur(
    n_ctx,
    seq_len,
    rows_ref,
    meta_ref,
    lens_ref,
    rate_ref,
    gain_ref,
    mix_ref,
    bonus_ref,
    scale_ref,
    shift_ref,
    out_ref,
    trans,
    push,
    keep,
    carry_out,
    local_out,
    values,
    state,
):
    ctx = lax.axis_index("context")
    odd = lax.rem(ctx, 2) == 1

    def head_row(ref):
        line = ref[pl.ds(ctx // 2, 1), :]
        return jnp.where(odd, line[:, SPAN:], line[:, :SPAN])

    rate, gain, mix = head_row(rate_ref), head_row(gain_ref), head_row(mix_ref)
    bonus, scale, shift = head_row(bonus_ref), head_row(scale_ref), head_row(shift_ref)
    first = lens_ref[0, 0]
    second = first + lens_ref[0, 1]
    third = second + lens_ref[0, 2]

    def doc_of(position):
        return (
            (position >= first).astype(jnp.int32)
            + (position >= second).astype(jnp.int32)
            + (position >= third).astype(jnp.int32)
        )

    n_src = rows_ref.shape[0]
    block = meta_ref.shape[2]
    half = rows_ref.shape[1] // 2
    notes = meta_ref[...].reshape(n_ctx * 8, block).T
    row_i = lax.broadcasted_iota(jnp.int32, (CHUNK, CHUNK), 0)
    col_i = lax.broadcasted_iota(jnp.int32, (CHUNK, CHUNK), 1)
    tri = (row_i >= col_i).astype(bf16)
    tri3 = jnp.concatenate([tri, tri, tri], axis=1)
    eye = (row_i == col_i).astype(f32)
    within = {}
    size = SMALL
    while size <= CHUNK:
        within[size] = (row_i // size) == (col_i // size)
        size *= 2
    blocks_per_group = GROUP * CHUNK // block

    for group in range(seq_len // (GROUP * CHUNK)):
        base = group * GROUP * CHUNK
        span = GROUP * CHUNK
        phase = group * blocks_per_group // (n_ctx // 2)
        source = rows_ref[:, phase * half : (phase + 1) * half, :].reshape(n_src * half, 4 * SPAN)
        taken, codes = [], []
        for b in range(blocks_per_group):
            c = group * blocks_per_group + b
            pointer = notes[:, c * 8 : c * 8 + 1].astype(jnp.int32)
            where = (pointer // 128) * half + lax.rem(pointer, half)
            pick = (
                lax.broadcasted_iota(jnp.int32, (block, n_src * half), 1) == where
            ).astype(bf16)
            taken.append(nn(pick, source))
            codes.append(notes[:, c * 8 + 1 : c * 8 + 2])
        taken = jnp.concatenate(taken, axis=0)
        code = jnp.concatenate(codes, axis=0)
        r, k = taken[:, :SPAN], taken[:, SPAN : 2 * SPAN]
        v, a = taken[:, 2 * SPAN : 3 * SPAN], taken[:, 3 * SPAN :]
        position = base + lax.broadcasted_iota(jnp.int32, (span, 1), 0)
        doc = doc_of(position)
        starts = doc != doc_of(position - 1)
        before = doc_of(position - lax.rem(position, CHUNK) - 1)
        last = doc_of(position - lax.rem(position, CHUNK) + (CHUNK - 1))
        scaled = k * gain
        unit = scaled * lax.rsqrt(jnp.sum(scaled * scaled, axis=1, keepdims=True) + unit_eps)
        mixed = k * (1.0 + (a - 1.0) * mix)
        erase = jnp.where(starts, 0.0, unit * a)
        extra = jnp.sum(r * mixed * bonus, axis=1, keepdims=True) * v
        decay = -decay_cap * (1.0 - jnp.exp(-rate * code))
        d0 = decay.astype(bf16)
        rest = decay - d0.astype(f32)
        d1 = rest.astype(bf16)
        d2 = (rest - d1.astype(f32)).astype(bf16)
        cums, lasts = [], []
        for j in range(GROUP):
            s = slice(j * CHUNK, (j + 1) * CHUNK)
            cum = nn(tri3, jnp.concatenate([d0[s], d1[s], d2[s]], axis=0))
            cums.append(cum)
            lasts.append(jnp.broadcast_to(cum[CHUNK - 1 :], (CHUNK, SPAN)))
        cum = jnp.concatenate(cums, axis=0)
        end = jnp.concatenate(lasts, axis=0)
        up = jnp.exp(cum)
        down = jnp.exp(-cum)
        unit_up = unit * jnp.exp(cum - decay)
        recept_up = r * up
        erase_down = erase * down
        mixed_down = mixed * down
        alive = doc == before
        unit_start = jnp.where(alive, unit_up, 0.0)
        recept_start = jnp.where(alive, recept_up, 0.0)
        tail = jnp.where(doc == last, jnp.exp(end - cum), 0.0)
        erase_tail = erase * tail
        mixed_tail = mixed * tail
        for j in range(GROUP):
            s = slice(j * CHUNK, (j + 1) * CHUNK)
            chunk = group * GROUP + j
            doc_row = doc_of(
                base + j * CHUNK + lax.broadcasted_iota(jnp.int32, (1, CHUNK), 1)
            )
            same = doc[s] == doc_row
            strict = same & (row_i > col_i)
            inclusive = same & (row_i >= col_i)
            scores = nt(
                jnp.concatenate([unit_up[s], recept_up[s]], axis=0),
                jnp.concatenate([erase_down[s], mixed_down[s]], axis=0),
            )
            erase_mat = jnp.where(strict, scores[:CHUNK, :CHUNK], 0.0)
            write_mat = jnp.where(strict, scores[:CHUNK, CHUNK:], 0.0)
            read_erase = jnp.where(inclusive, scores[CHUNK:, :CHUNK], 0.0)
            read_write = jnp.where(inclusive, scores[CHUNK:, CHUNK:], 0.0)
            power = jnp.where(within[SMALL], -erase_mat, 0.0)
            inverse = eye + power
            size = 2
            while size < SMALL:
                power = nn(power, power)
                inverse = inverse + nn(inverse, power)
                size *= 2
            size = SMALL
            while size < CHUNK:
                off = jnp.where(within[2 * size] & ~within[size], erase_mat, 0.0)
                inverse = inverse - nn(inverse, nn(off, inverse))
                size *= 2
            value = v[s]
            both = nn(jnp.concatenate([write_mat, read_write], axis=0), value)
            solved = nn(inverse, jnp.concatenate([both[:CHUNK], unit_start[s]], axis=1))
            read = nn(read_erase, solved)
            local_out[chunk] = both[CHUNK:] - read[:, :SPAN] + extra[s]
            carry_out[chunk] = (recept_start[s] - read[:, SPAN:]).astype(bf16)
            moved = tn(solved, erase_tail[s])
            trans[chunk] = moved[SPAN:].astype(bf16)
            push[chunk] = tn(value, mixed_tail[s]) - moved[:SPAN]
            ends = jnp.exp(cums[j][CHUNK - 1 :])
            alive_end = doc_of(base + j * CHUNK + CHUNK - 1) == doc_of(base + j * CHUNK - 1)
            keep[chunk] = jnp.broadcast_to(jnp.where(alive_end, ends, 0.0), (8, SPAN))

    n_chunks = seq_len // CHUNK

    def advance(chunk, now):
        state[chunk] = now.astype(bf16)
        return now * keep[chunk][0:1] - nn(now, trans[chunk]) + push[chunk]

    lax.fori_loop(0, n_chunks, advance, jnp.zeros((SPAN, SPAN), f32))

    def finish(index, carry):
        lines = []
        for j in range(2):
            chunk = index * 2 + j
            whole = nt(carry_out[chunk], state[chunk]) + local_out[chunk]
            center = whole - jnp.mean(whole, axis=1, keepdims=True)
            spread = jnp.mean(center * center, axis=1, keepdims=True)
            lines.append(center * lax.rsqrt(spread + group_eps) * scale + shift)
        out_ref[index] = jnp.concatenate(lines, axis=1).astype(bf16)
        return carry

    lax.fori_loop(0, n_chunks // 2, finish, 0)


def vmem():
    return pl.BlockSpec(memory_space=pltpu.VMEM)


def run_recur(n_ctx, seq_len, block, rows, meta, lens, vectors):
    n_chunks = seq_len // CHUNK
    return pl.pallas_call(
        functools.partial(recur, n_ctx, seq_len),
        out_shape=jax.ShapeDtypeStruct((n_ctx, block // 2, 2 * SPAN), bf16),
        in_specs=[vmem(), vmem(), pl.BlockSpec(memory_space=pltpu.SMEM)] + [vmem()] * 6,
        out_specs=vmem(),
        scratch_shapes=[
            pltpu.VMEM((n_chunks, SPAN, SPAN), bf16),
            pltpu.VMEM((n_chunks, SPAN, SPAN), f32),
            pltpu.VMEM((n_chunks, 8, SPAN), f32),
            pltpu.VMEM((n_chunks, CHUNK, SPAN), bf16),
            pltpu.VMEM((n_chunks, CHUNK, SPAN), f32),
            pltpu.VMEM((8, 128), f32),
            pltpu.VMEM((n_chunks, SPAN, SPAN), bf16),
        ],
        compiler_params=pltpu.CompilerParams(vmem_limit_bytes=48 << 20),
    )(rows, meta, lens, *vectors)


def local(
    acceptance_vectors,
    lookup_vectors,
    payload_vectors,
    incontext_adaptation,
    fading_codes,
    stacked_line_pointer,
    article_extents,
    feature_fading,
    erasure_lookup_scaling,
    lookup_mixture_share,
    reward_coefficients,
    cluster_standard_scaling,
    cluster_standard_offset,
    final_projection,
):
    tokens, features = acceptance_vectors.shape
    n_dp = lax.axis_size("dp")
    n_ctx = lax.axis_size("context")
    n_peers = n_dp * n_ctx
    per_seq = tokens // n_dp
    seq_len = tokens * n_ctx
    rows, meta = pl.pallas_call(
        functools.partial(exchange, n_ctx, n_peers, per_seq),
        out_shape=(
            jax.ShapeDtypeStruct((n_peers, per_seq, 4 * SPAN), bf16),
            jax.ShapeDtypeStruct((n_ctx, 8, tokens), f32),
        ),
        in_specs=[vmem()] * 6,
        out_specs=(vmem(), vmem()),
        scratch_shapes=[
            pltpu.VMEM((n_peers, per_seq, 4 * SPAN), bf16),
            pltpu.VMEM((n_ctx, 8, tokens), f32),
            pltpu.SemaphoreType.DMA,
            pltpu.SemaphoreType.DMA,
            pltpu.SemaphoreType.DMA,
            pltpu.SemaphoreType.DMA,
            pltpu.SemaphoreType.DMA((2,)),
        ],
        compiler_params=pltpu.CompilerParams(
            collective_id=0, has_side_effects=True, vmem_limit_bytes=32 << 20
        ),
    )(
        acceptance_vectors,
        lookup_vectors,
        payload_vectors,
        incontext_adaptation,
        fading_codes[0],
        stacked_line_pointer,
    )
    vectors = [
        item.reshape(features // 128, 128)
        for item in (
            feature_fading,
            erasure_lookup_scaling,
            lookup_mixture_share,
            reward_coefficients,
            cluster_standard_scaling,
            cluster_standard_offset,
        )
    ]
    normed = run_recur(n_ctx, seq_len, tokens, rows, meta, article_extents, vectors)
    heads = lax.all_to_all(normed, "context", split_axis=0, concat_axis=0, tiled=True)
    lines = (
        heads.reshape(n_ctx, tokens // 2, 2, SPAN).transpose(2, 1, 0, 3).reshape(tokens, features)
    )
    summed = lax.psum_scatter(
        jnp.dot(lines, final_projection, preferred_element_type=f32).astype(bf16),
        "tensor",
        scatter_dimension=0,
        tiled=True,
    )
    return summed.reshape(1, tokens // lax.axis_size("tensor"), final_projection.shape[1])


def solution(mesh):
    return jax.shard_map(
        local,
        mesh=mesh,
        in_specs=(
            P(("dp", "context"), "tensor"),
            P(("dp", "context"), "tensor"),
            P(("dp", "context"), "tensor"),
            P(("dp", "context"), "tensor"),
            P("dp", "context", "tensor"),
            P("dp", "context"),
            P("dp", None),
            P("tensor"),
            P("tensor"),
            P("tensor"),
            P("tensor"),
            P("tensor"),
            P("tensor"),
            P("tensor", None),
        ),
        out_specs=P("dp", ("context", "tensor"), None),
        check_vma=False,
    )
```

```python
import functools

import jax
import jax.numpy as jnp
from jax import lax
from jax.experimental import pallas as pl
from jax.experimental.pallas import tpu as pltpu
from jax.sharding import PartitionSpec as P

MESH = pl.DeviceIdType.MESH
SPAN = 64
GROUP = 4
SMALL = 8
decay_cap = 0.606531
unit_eps = 1e-06
group_eps = 0.00064
f32 = jnp.float32
bf16 = jnp.bfloat16


def nn(a, b):
    return lax.dot_general(
        a.astype(bf16), b.astype(bf16), (((1,), (0,)), ((), ())), preferred_element_type=f32
    )


def nt(a, b):
    return lax.dot_general(
        a.astype(bf16), b.astype(bf16), (((1,), (1,)), ((), ())), preferred_element_type=f32
    )


def tn(a, b):
    return lax.dot_general(
        a.astype(bf16), b.astype(bf16), (((0,), (0,)), ((), ())), preferred_element_type=f32
    )


def exchange(
    n_ctx,
    n_peers,
    per_seq,
    r_ref,
    k_ref,
    v_ref,
    a_ref,
    code_ref,
    ptr_ref,
    rows_ref,
    meta_ref,
    packed,
    notes,
    send_sem,
    recv_sem,
    note_send,
    note_recv,
    own_sem,
):
    dp = lax.axis_index("dp")
    ctx = lax.axis_index("context")
    me = dp * n_ctx + ctx
    tensor = lax.axis_index("tensor")

    def place(index):
        return (index // n_ctx, lax.rem(index, n_ctx), tensor)

    barrier = pltpu.get_barrier_semaphore()

    def greet(step, carry):
        other = lax.rem(me + step, n_peers)
        pl.semaphore_signal(barrier, inc=1, device_id=place(other), device_id_type=MESH)
        return carry

    lax.fori_loop(1, n_peers, greet, 0)

    tokens = r_ref.shape[0]
    n_dp = n_peers // n_ctx
    for pair in range(n_ctx // 2):
        lanes = slice(128 * pair, 128 * pair + 128)
        left, right = slice(0, SPAN), slice(SPAN, 128)
        r, k, v, a = r_ref[:, lanes], k_ref[:, lanes], v_ref[:, lanes], a_ref[:, lanes]
        for half, part in ((0, left), (1, right)):
            rk = jnp.concatenate([r[:, part], k[:, part]], axis=1)
            va = jnp.concatenate([v[:, part], a[:, part]], axis=1)
            for s in range(n_dp):
                slot = s * n_ctx + 2 * pair + half
                packed[slot, :, 0:128] = rk[s * per_seq : (s + 1) * per_seq]
                packed[slot, :, 128:256] = va[s * per_seq : (s + 1) * per_seq]

    eye = (
        lax.broadcasted_iota(jnp.int32, (tokens, tokens), 0)
        == lax.broadcasted_iota(jnp.int32, (tokens, tokens), 1)
    ).astype(f32)
    codes = lax.dot_general(
        code_ref[...].astype(f32),
        eye,
        (((0,), (0,)), ((), ())),
        precision=lax.Precision.HIGHEST,
        preferred_element_type=f32,
    )
    pointers = ptr_ref[...].astype(f32)
    for c in range(n_ctx):
        notes[c, 0:1, :] = pointers
        notes[c, 1:2, :] = codes[c : c + 1, :]
        notes[c, 2:8, :] = jnp.zeros((6, tokens), f32)

    pl.semaphore_wait(barrier, n_peers - 1)

    own_rows = pltpu.make_async_copy(packed.at[me], rows_ref.at[me], own_sem.at[0])
    own_rows.start()
    own_note = pltpu.make_async_copy(notes.at[ctx], meta_ref.at[ctx], own_sem.at[1])
    own_note.start()

    def note_copy(step):
        other = lax.rem(ctx + step, n_ctx)
        return pltpu.make_async_remote_copy(
            src_ref=notes.at[other],
            dst_ref=meta_ref.at[ctx],
            send_sem=note_send,
            recv_sem=note_recv,
            device_id=(dp, other, tensor),
            device_id_type=MESH,
        )

    def rows_copy(step):
        other = lax.rem(me + step, n_peers)
        return pltpu.make_async_remote_copy(
            src_ref=packed.at[other],
            dst_ref=rows_ref.at[me],
            send_sem=send_sem,
            recv_sem=recv_sem,
            device_id=place(other),
            device_id_type=MESH,
        )

    def send_note(step, carry):
        note_copy(step).start()
        return carry

    def send_rows(step, carry):
        rows_copy(step).start()
        return carry

    lax.fori_loop(1, n_ctx, send_note, 0)
    lax.fori_loop(1, n_peers, send_rows, 0)
    own_rows.wait()
    own_note.wait()
    rest_rows = rows_ref.at[pl.ds(0, n_peers - 1)]
    rest_notes = meta_ref.at[pl.ds(0, n_ctx - 1)]
    pltpu.make_async_copy(rest_notes, rest_notes, note_send).wait()
    pltpu.make_async_copy(rest_notes, rest_notes, note_recv).wait()
    pltpu.make_async_copy(rest_rows, rest_rows, send_sem).wait()
    pltpu.make_async_copy(rest_rows, rest_rows, recv_sem).wait()


def recur(
    n_ctx,
    seq_len,
    rows_ref,
    meta_ref,
    lens_ref,
    rate_ref,
    gain_ref,
    mix_ref,
    bonus_ref,
    scale_ref,
    shift_ref,
    out_ref,
    wide_rk,
    wide_va,
):
    ctx = lax.axis_index("context")
    odd = lax.rem(ctx, 2) == 1
    n_src, per_seq = rows_ref.shape[0], rows_ref.shape[1]
    block = meta_ref.shape[2]
    lane = lax.broadcasted_iota(jnp.int32, (block, block), 1)
    row = lax.broadcasted_iota(jnp.int32, (block, block), 0)
    flip = (lane[:SPAN] & (SPAN - 1)) == row[:SPAN]

    lines = []
    for ref in (rate_ref, gain_ref, mix_ref, bonus_ref, scale_ref, shift_ref):
        lines.append(ref[pl.ds(ctx // 2, 1), :])
    lines = jnp.concatenate(lines + lines[:2], axis=0)
    lines = jnp.where(odd, lines[:, SPAN:], lines[:, :SPAN])

    def column(index):
        line = jnp.broadcast_to(lines[index : index + 1], (SPAN, SPAN))
        return jnp.sum(jnp.where(flip[:, :SPAN], line, 0.0), axis=1, keepdims=True) + jnp.zeros(
            (SPAN, block), f32
        )

    rate, gain, mix, bonus, scale, shift = [column(index) for index in range(6)]
    first = lens_ref[0, 0]
    second = first + lens_ref[0, 1]
    third = second + lens_ref[0, 2]

    def doc_start(position):
        found = jnp.where(position >= first, first, 0)
        found = jnp.where(position >= second, second, found)
        return jnp.where(position >= third, third, found)

    spread = rows_ref[...].reshape(n_src * per_seq, 4 * SPAN).astype(f32)
    wide_rk[...] = spread[:, : 2 * SPAN]
    wide_va[...] = spread[:, 2 * SPAN :]

    mid = block // 2
    sums = jnp.concatenate(
        [
            (row <= lane).astype(f32) - (row < mid).astype(f32),
            (row >= mid).astype(f32),
            (row < mid).astype(f32),
        ],
        axis=1,
    ).astype(bf16)
    eye = (row == lane).astype(f32)
    nbits = {}
    size = SMALL
    while size <= block:
        nbits[size] = (row // size) == (lane // size)
        size *= 2

    now = jnp.zeros((SPAN, SPAN), f32)
    for group in range(n_ctx // GROUP):
        ids = [group * GROUP + b for b in range(GROUP)]
        each = range(GROUP)
        got = []
        for c in ids:
            pointer = meta_ref[c, 0:1, :].astype(jnp.int32)
            where = (pointer & 1) * n_src + (pointer // 128)
            pick = (row == where).astype(bf16)
            parts = []
            for wide in (wide_rk, wide_va):
                even = wide[pl.ds(2 * c, n_src, stride=per_seq), :]
                uneven = wide[pl.ds(2 * c + 1, n_src, stride=per_seq), :]
                parts.append(jnp.concatenate([even, uneven], axis=0).T)
            got.append(nn(jnp.concatenate(parts, axis=0), pick))
        r = [g[:SPAN] for g in got]
        k = [g[SPAN : 2 * SPAN] for g in got]
        v = [g[2 * SPAN : 3 * SPAN] for g in got]
        a = [g[3 * SPAN :] for g in got]
        position = [c * block + lane[0:1] for c in ids]
        start = [doc_start(p) for p in position]
        start_last = [doc_start(c * block + block - 1) for c in ids]
        decay = [
            -decay_cap * (1.0 - jnp.exp(-rate * meta_ref[c, 1:2, :])) for c in ids
        ]
        cums = []
        for d in decay:
            d0 = d.astype(bf16)
            rest = d - d0.astype(f32)
            d1 = rest.astype(bf16)
            d2 = (rest - d1.astype(f32)).astype(bf16)
            total = nn(jnp.concatenate([d0, d1, d2], axis=0), sums)
            cums.append(total[:SPAN] + total[SPAN : 2 * SPAN] + total[2 * SPAN :])
        about = [x[:, :block] for x in cums]
        to_end = [x[:, block : 2 * block] for x in cums]
        to_mid = [x[:, 2 * block :] for x in cums]
        scaled = [x * gain for x in k]
        unit = [
            x * lax.rsqrt(jnp.sum(x * x, axis=0, keepdims=True) + unit_eps) for x in scaled
        ]
        mixed = [k[i] * (1.0 + (a[i] - 1.0) * mix) for i in each]
        erase = [jnp.where(start[i] == position[i], 0.0, unit[i] * a[i]) for i in each]
        extra = [
            jnp.sum(r[i] * mixed[i] * (bonus + 1.0), axis=0, keepdims=True) * v[i] for i in each
        ]
        down = [jnp.exp(-x) for x in about]
        unit_up = [unit[i] * jnp.exp(about[i] - decay[i]) for i in each]
        recept_up = [r[i] * jnp.exp(about[i]) for i in each]
        opening = [
            jnp.where(start[i] < ids[i] * block, jnp.exp(to_mid[i]), 0.0) for i in each
        ]
        unit_start = [unit_up[i] * opening[i] for i in each]
        recept_start = [recept_up[i] * opening[i] for i in each]
        erase_down = [(erase[i] * down[i]).T.astype(bf16) for i in each]
        mixed_down = [(mixed[i] * down[i]).T.astype(bf16) for i in each]
        ends = []
        for i in each:
            choice = jnp.where(lane[:SPAN] < SPAN, to_end[i], to_end[i] + to_mid[i])
            ends.append(jnp.exp(jnp.sum(jnp.where(flip, choice, 0.0), axis=0, keepdims=True)))
        fade = [x[:, :SPAN] for x in ends]
        keep = [
            jnp.where(start_last[i] < ids[i] * block, ends[i][:, SPAN:], 0.0) for i in each
        ]
        scores = [
            nn(
                jnp.concatenate([erase_down[i], mixed_down[i]], axis=0),
                jnp.concatenate([unit_up[i], recept_up[i]], axis=1),
            )
            for i in each
        ]
        inside = [row >= start[i] - ids[i] * block for i in each]
        strict = [inside[i] & (row < lane) for i in each]
        inclusive = [inside[i] & (row <= lane) for i in each]
        erase_mat = [jnp.where(strict[i], scores[i][:block, :block], 0.0) for i in each]
        read_erase = [
            jnp.where(inclusive[i], scores[i][:block, block:], 0.0).astype(bf16) for i in each
        ]
        write_mat = [
            jnp.where(strict[i], scores[i][block:, :block], 0.0).astype(bf16) for i in each
        ]
        read_write = [
            jnp.where(strict[i], scores[i][block:, block:], 0.0).astype(bf16) for i in each
        ]
        power = [jnp.where(nbits[SMALL], -x, 0.0) for x in erase_mat]
        inverse = [eye + x for x in power]
        size = 2
        while size < SMALL:
            power = [nn(x, x) for x in power]
            inverse = [inverse[i] + nn(inverse[i], power[i]) for i in each]
            size *= 2
        size = SMALL
        while size < block:
            ring = nbits[2 * size] & ~nbits[size]
            inner = [nn(jnp.where(ring, erase_mat[i], 0.0), inverse[i]) for i in each]
            inverse = [inverse[i] - nn(inverse[i], inner[i]) for i in each]
            size *= 2
        both = [
            nn(v[i], jnp.concatenate([write_mat[i], read_write[i]], axis=1)) for i in each
        ]
        solved = [
            nn(jnp.concatenate([both[i][:, :block], unit_start[i]], axis=0), inverse[i])
            for i in each
        ]
        read = [nn(solved[i], read_erase[i]) for i in each]
        local_out = [both[i][:, block:] - read[i][:SPAN] + extra[i] for i in each]
        carry_out = [(recept_start[i] - read[i][SPAN:]).astype(bf16) for i in each]
        last = [start[i] == start_last[i] for i in each]
        moved = [nn(jnp.where(last[i], solved[i], 0.0), erase_down[i]) for i in each]
        put = [nn(jnp.where(last[i], v[i], 0.0), mixed_down[i]) for i in each]
        push = [(put[i] - moved[i][:SPAN]) * fade[i] for i in each]
        trans = [(moved[i][SPAN:] * fade[i]).astype(bf16) for i in each]
        whole = []
        for i in each:
            carried = now.astype(bf16)
            whole.append(nn(carried, carry_out[i]) + local_out[i])
            now = now * keep[i] - nn(carried, trans[i]) + push[i]
        for i in each:
            center = whole[i] - jnp.mean(whole[i], axis=0, keepdims=True)
            power2 = jnp.mean(center * center, axis=0, keepdims=True)
            out_ref[ids[i]] = (center * lax.rsqrt(power2 + group_eps) * scale + shift).astype(bf16)


def vmem():
    return pl.BlockSpec(memory_space=pltpu.VMEM)


def run_recur(n_ctx, seq_len, block, rows, meta, lens, vectors):
    return pl.pallas_call(
        functools.partial(recur, n_ctx, seq_len),
        out_shape=jax.ShapeDtypeStruct((n_ctx, SPAN, block), bf16),
        in_specs=[vmem(), vmem(), pl.BlockSpec(memory_space=pltpu.SMEM)] + [vmem()] * 6,
        out_specs=vmem(),
        scratch_shapes=[
            pltpu.VMEM((seq_len, 2 * SPAN), f32),
            pltpu.VMEM((seq_len, 2 * SPAN), f32),
        ],
        compiler_params=pltpu.CompilerParams(vmem_limit_bytes=48 << 20),
    )(rows, meta, lens, *vectors)


def project(
    n_ctx,
    n_tensor,
    normed_ref,
    weight_ref,
    out_ref,
    weight,
    heads,
    parts,
    landed,
    load_sem,
    own_sem,
    head_send,
    head_recv,
    part_send,
    part_recv,
):
    dp = lax.axis_index("dp")
    ctx = lax.axis_index("context")
    tensor = lax.axis_index("tensor")
    barrier = pltpu.get_barrier_semaphore()
    n_parts, width = weight.shape[0], weight.shape[2]

    def load(n):
        return pltpu.make_async_copy(
            weight_ref.at[:, pl.ds(n * width, width)], weight.at[n], load_sem.at[n]
        )

    def greet(step, carry):
        other = lax.rem(ctx + step, n_ctx)
        pl.semaphore_signal(barrier, inc=1, device_id=(dp, other, tensor), device_id_type=MESH)
        return carry

    lax.fori_loop(1, n_ctx, greet, 0)
    for step in range(1, n_tensor):
        other = lax.rem(tensor + step, n_tensor)
        pl.semaphore_signal(barrier, inc=1, device_id=(dp, ctx, other), device_id_type=MESH)
    for n in range(n_parts):
        load(n).start()
    pl.semaphore_wait(barrier, n_ctx - 1 + n_tensor - 1)

    own = pltpu.make_async_copy(normed_ref.at[ctx], heads.at[ctx], own_sem)
    own.start()

    def send(step, carry):
        other = lax.rem(ctx + step, n_ctx)
        pltpu.make_async_remote_copy(
            src_ref=normed_ref.at[other],
            dst_ref=heads.at[ctx],
            send_sem=head_send,
            recv_sem=head_recv,
            device_id=(dp, other, tensor),
            device_id_type=MESH,
        ).start()
        return carry

    lax.fori_loop(1, n_ctx, send, 0)
    own.wait()
    rest = heads.at[pl.ds(0, n_ctx - 1)]
    pltpu.make_async_copy(rest, rest, head_recv).wait()
    lines = jnp.concatenate(
        [
            heads[2 * c : 2 * c + 2].reshape(2 * SPAN, heads.shape[2]).T
            for c in range(n_ctx // 2)
        ],
        axis=1,
    )

    def part_copy(n, step):
        other = lax.rem(tensor + step, n_tensor)
        return pltpu.make_async_remote_copy(
            src_ref=parts.at[n, other],
            dst_ref=landed.at[n, step - 1],
            send_sem=part_send.at[n, step - 1],
            recv_sem=part_recv.at[n, step - 1],
            device_id=(dp, ctx, other),
            device_id_type=MESH,
        )

    own_rows = parts.shape[2]
    for n in range(n_parts):
        load(n).wait()
        product = jnp.dot(lines, weight[n], preferred_element_type=f32).astype(bf16)
        for q in range(n_tensor):
            parts[n, q] = product[q * own_rows : (q + 1) * own_rows]
        for step in (2, 1, 3):
            part_copy(n, step).start()
    for n in range(n_parts):
        total = parts[n, tensor].astype(f32)
        for step in range(1, n_tensor):
            part_copy(n, step).wait_recv()
            total = total + landed[n, step - 1].astype(f32)
        out_ref[:, n * width : (n + 1) * width] = total.astype(bf16)
    pltpu.make_async_copy(rest, rest, head_send).wait()
    for n in range(n_parts):
        for step in range(1, n_tensor):
            part_copy(n, step).wait_send()


def run_project(n_ctx, n_tensor, tokens, normed, weight):
    depth, columns = weight.shape
    n_parts = 4
    own_rows = tokens // n_tensor
    width = columns // n_parts
    return pl.pallas_call(
        functools.partial(project, n_ctx, n_tensor),
        out_shape=jax.ShapeDtypeStruct((own_rows, columns), bf16),
        in_specs=[vmem(), pl.BlockSpec(memory_space=pl.ANY)],
        out_specs=vmem(),
        scratch_shapes=[
            pltpu.VMEM((n_parts, depth, width), bf16),
            pltpu.VMEM((n_ctx, SPAN, tokens), bf16),
            pltpu.VMEM((n_parts, n_tensor, own_rows, width), bf16),
            pltpu.VMEM((n_parts, n_tensor - 1, own_rows, width), bf16),
            pltpu.SemaphoreType.DMA((n_parts,)),
            pltpu.SemaphoreType.DMA,
            pltpu.SemaphoreType.DMA,
            pltpu.SemaphoreType.DMA,
            pltpu.SemaphoreType.DMA((n_parts, n_tensor - 1)),
            pltpu.SemaphoreType.DMA((n_parts, n_tensor - 1)),
        ],
        compiler_params=pltpu.CompilerParams(
            collective_id=1, has_side_effects=True, vmem_limit_bytes=48 << 20
        ),
    )(normed, weight)


def local(
    acceptance_vectors,
    lookup_vectors,
    payload_vectors,
    incontext_adaptation,
    fading_codes,
    stacked_line_pointer,
    article_extents,
    feature_fading,
    erasure_lookup_scaling,
    lookup_mixture_share,
    reward_coefficients,
    cluster_standard_scaling,
    cluster_standard_offset,
    final_projection,
):
    tokens, features = acceptance_vectors.shape
    n_dp = lax.axis_size("dp")
    n_ctx = lax.axis_size("context")
    n_peers = n_dp * n_ctx
    per_seq = tokens // n_dp
    seq_len = tokens * n_ctx
    rows, meta = pl.pallas_call(
        functools.partial(exchange, n_ctx, n_peers, per_seq),
        out_shape=(
            jax.ShapeDtypeStruct((n_peers, per_seq, 4 * SPAN), bf16),
            jax.ShapeDtypeStruct((n_ctx, 8, tokens), f32),
        ),
        in_specs=[vmem()] * 6,
        out_specs=(vmem(), vmem()),
        scratch_shapes=[
            pltpu.VMEM((n_peers, per_seq, 4 * SPAN), bf16),
            pltpu.VMEM((n_ctx, 8, tokens), f32),
            pltpu.SemaphoreType.DMA,
            pltpu.SemaphoreType.DMA,
            pltpu.SemaphoreType.DMA,
            pltpu.SemaphoreType.DMA,
            pltpu.SemaphoreType.DMA((2,)),
        ],
        compiler_params=pltpu.CompilerParams(
            collective_id=0, has_side_effects=True, vmem_limit_bytes=32 << 20
        ),
    )(
        acceptance_vectors,
        lookup_vectors,
        payload_vectors,
        incontext_adaptation,
        fading_codes[0],
        stacked_line_pointer,
    )
    vectors = [
        item.reshape(features // 128, 128)
        for item in (
            feature_fading,
            erasure_lookup_scaling,
            lookup_mixture_share,
            reward_coefficients,
            cluster_standard_scaling,
            cluster_standard_offset,
        )
    ]
    normed = run_recur(n_ctx, seq_len, tokens, rows, meta, article_extents, vectors)
    n_tensor = lax.axis_size("tensor")
    summed = run_project(n_ctx, n_tensor, tokens, normed, final_projection)
    return summed.reshape(1, tokens // n_tensor, final_projection.shape[1])


def solution(mesh):
    return jax.shard_map(
        local,
        mesh=mesh,
        in_specs=(
            P(("dp", "context"), "tensor"),
            P(("dp", "context"), "tensor"),
            P(("dp", "context"), "tensor"),
            P(("dp", "context"), "tensor"),
            P("dp", "context", "tensor"),
            P("dp", "context"),
            P("dp", None),
            P("tensor"),
            P("tensor"),
            P("tensor"),
            P("tensor"),
            P("tensor"),
            P("tensor"),
            P("tensor", None),
        ),
        out_specs=P("dp", ("context", "tensor"), None),
        check_vma=False,
    )
```

```python
import functools

import jax
import jax.numpy as jnp
from jax import lax
from jax.experimental import pallas as pl
from jax.experimental.pallas import tpu as pltpu
from jax.sharding import PartitionSpec as P

MESH = pl.DeviceIdType.MESH
SPAN = 64
GROUP = 4
SMALL = 8
PARTS = 4
decay_cap = 0.606531
unit_eps = 1e-06
group_eps = 0.00064
f32 = jnp.float32
bf16 = jnp.bfloat16


def nn(a, b):
    return lax.dot_general(
        a.astype(bf16), b.astype(bf16), (((1,), (0,)), ((), ())), preferred_element_type=f32
    )


def layer(
    n_dp,
    n_ctx,
    n_tensor,
    r_hbm,
    k_hbm,
    v_hbm,
    a_hbm,
    code_hbm,
    ptr_hbm,
    lens_hbm,
    rate_hbm,
    gain_hbm,
    mix_hbm,
    bonus_hbm,
    scale_hbm,
    shift_hbm,
    weight_hbm,
    out_ref,
    r_ref,
    k_ref,
    v_ref,
    a_ref,
    code_ref,
    ptr_ref,
    lens_ref,
    lines_ref,
    weight,
    packed,
    rows,
    wide,
    notes,
    meta,
    pre,
    tips,
    picks,
    normed,
    heads,
    parts,
    landed,
    load_sem,
    weight_sem,
    own_sem,
    note_send,
    note_recv,
    rows_send,
    rows_recv,
    head_send,
    head_recv,
    part_send,
    part_recv,
):
    dp = lax.axis_index("dp")
    ctx = lax.axis_index("context")
    tensor = lax.axis_index("tensor")
    n_peers = n_dp * n_ctx
    me = dp * n_ctx + ctx
    block = r_ref.shape[0]
    n_groups = n_ctx // GROUP
    width = weight.shape[2]

    loads = [
        (r_hbm, r_ref),
        (k_hbm, k_ref),
        (v_hbm, v_ref),
        (a_hbm, a_ref),
        (code_hbm, code_ref),
        (ptr_hbm, ptr_ref),
        (lens_hbm, lens_ref),
    ]
    for i, ref in enumerate((rate_hbm, gain_hbm, mix_hbm, bonus_hbm, scale_hbm, shift_hbm)):
        loads.append((ref, lines_ref.at[i]))
    loads = [
        pltpu.make_async_copy(src, dst, load_sem.at[i]) for i, (src, dst) in enumerate(loads)
    ]
    for load in loads:
        load.start()

    def place(index):
        return (index // n_ctx, lax.rem(index, n_ctx), tensor)

    barrier = pltpu.get_barrier_semaphore()

    def greet(step, carry):
        other = lax.rem(me + step, n_peers)
        pl.semaphore_signal(barrier, inc=1, device_id=place(other), device_id_type=MESH)
        return carry

    lax.fori_loop(1, n_peers, greet, 0)
    for step in range(1, n_tensor):
        other = lax.rem(tensor + step, n_tensor)
        pl.semaphore_signal(barrier, inc=1, device_id=(dp, ctx, other), device_id_type=MESH)

    def weight_load(n):
        return pltpu.make_async_copy(
            weight_hbm.at[:, pl.ds(n * width, width)], weight.at[n], weight_sem.at[n]
        )

    for load in loads:
        load.wait()
    for n in range(PARTS):
        weight_load(n).start()

    per_seq = block // n_dp
    for pair in range(n_ctx // 2):
        lanes = slice(128 * pair, 128 * pair + 128)
        r, k, v, a = r_ref[:, lanes], k_ref[:, lanes], v_ref[:, lanes], a_ref[:, lanes]
        for half, part in ((0, slice(0, SPAN)), (1, slice(SPAN, 128))):
            rk = jnp.concatenate([r[:, part], k[:, part]], axis=1).astype(f32)
            va = jnp.concatenate([v[:, part], a[:, part]], axis=1).astype(f32)
            for s in range(n_dp):
                slot = s * n_ctx + 2 * pair + half
                for g in range(n_groups):
                    piece = slice(s * per_seq + 8 * g, s * per_seq + 8 * g + 8)
                    packed[g, slot] = jnp.concatenate([rk[piece], va[piece]], axis=0).astype(bf16)
    codes = code_ref[...].astype(f32)
    pointers = ptr_ref[...].astype(f32)
    for c in range(n_ctx):
        notes[c] = jnp.concatenate(
            [pointers, codes[c : c + 1, :], jnp.zeros((6, block), f32)], axis=0
        )

    pl.semaphore_wait(barrier, n_peers - 1 + n_tensor - 1)

    own = [pltpu.make_async_copy(notes.at[ctx], meta.at[ctx], own_sem.at[n_groups])]
    for g in range(n_groups):
        own.append(pltpu.make_async_copy(packed.at[g, me], rows.at[g, me], own_sem.at[g]))
    for copy in own:
        copy.start()

    def send_note(step, carry):
        other = lax.rem(ctx + step, n_ctx)
        pltpu.make_async_remote_copy(
            src_ref=notes.at[other],
            dst_ref=meta.at[ctx],
            send_sem=note_send,
            recv_sem=note_recv,
            device_id=(dp, other, tensor),
            device_id_type=MESH,
        ).start()
        return carry

    lax.fori_loop(1, n_ctx, send_note, 0)
    for g in range(n_groups):

        def send_rows(step, carry, g=g):
            other = lax.rem(me + step, n_peers)
            pltpu.make_async_remote_copy(
                src_ref=packed.at[g, other],
                dst_ref=rows.at[g, me],
                send_sem=rows_send.at[g],
                recv_sem=rows_recv.at[g],
                device_id=place(other),
                device_id_type=MESH,
            ).start()
            return carry

        lax.fori_loop(1, n_peers, send_rows, 0)

    odd = lax.rem(ctx, 2) == 1
    lane = lax.broadcasted_iota(jnp.int32, (block, block), 1)
    row = lax.broadcasted_iota(jnp.int32, (block, block), 0)
    flip = (lane[:SPAN] & (SPAN - 1)) == row[:SPAN]

    def column(index):
        line = lines_ref[index, pl.ds(ctx // 2, 1), :]
        line = jnp.where(odd, line[:, SPAN:], line[:, :SPAN])
        line = jnp.broadcast_to(line, (SPAN, SPAN))
        return jnp.sum(jnp.where(flip[:, :SPAN], line, 0.0), axis=1, keepdims=True) + jnp.zeros(
            (SPAN, block), f32
        )

    rate, gain, mix, bonus, scale, shift = [column(index) for index in range(6)]
    lens = lens_ref[...]
    first = lens[:, 0:1]
    second = first + lens[:, 1:2]
    third = second + lens[:, 2:3]

    def doc_start(position):
        found = jnp.where(position >= first, first, 0)
        found = jnp.where(position >= second, second, found)
        return jnp.where(position >= third, third, found)

    mid = block // 2
    sums = jnp.concatenate(
        [
            (row <= lane).astype(f32) - (row < mid).astype(f32),
            (row >= mid).astype(f32),
            (row < mid).astype(f32),
        ],
        axis=1,
    ).astype(bf16)
    eye = (row == lane).astype(f32)
    nbits = {}
    size = SMALL
    while size <= block:
        nbits[size] = (row // size) == (lane // size)
        size *= 2
    own[0].wait()
    rest = meta.at[pl.ds(0, n_ctx - 1)]
    pltpu.make_async_copy(rest, rest, note_recv).wait()
    each = range(GROUP)
    for group in range(n_groups):
        ids = [group * GROUP + b for b in each]
        decay = [-decay_cap * (1.0 - jnp.exp(-rate * meta[c, 1:2, :])) for c in ids]
        cums = []
        for d in decay:
            d0 = d.astype(bf16)
            left = d - d0.astype(f32)
            d1 = left.astype(bf16)
            d2 = (left - d1.astype(f32)).astype(bf16)
            total = nn(jnp.concatenate([d0, d1, d2], axis=0), sums)
            cums.append(total[:SPAN] + total[SPAN : 2 * SPAN] + total[2 * SPAN :])
        for i, c in enumerate(ids):
            position = c * block + lane[0:1]
            start = doc_start(position)
            about = cums[i][:, :block]
            to_end = cums[i][:, block : 2 * block]
            to_mid = cums[i][:, 2 * block :]
            pre[c, 0] = jnp.exp(about)
            pre[c, 1] = jnp.exp(-about)
            pre[c, 2] = jnp.exp(about - decay[i])
            pre[c, 3] = jnp.where(start < c * block, jnp.exp(to_mid), 0.0)
            choice = jnp.where(lane[:SPAN] < SPAN, to_end, to_end + to_mid)
            ends = jnp.exp(jnp.sum(jnp.where(flip, choice, 0.0), axis=0, keepdims=True))
            through = doc_start(c * block + block - 1 + jnp.zeros((1, block), jnp.int32)) < c * block
            ends = jnp.where(through | (lane[0:1] < SPAN), ends, 0.0)
            tips[c] = jnp.broadcast_to(ends, (8, block))
            pointer = meta[c, 0:1, :].astype(jnp.int32)
            where = (pointer & 1) * n_peers + (pointer // block)
            picks[c] = (row == where).astype(bf16)

    def head_copy(c):
        return pltpu.make_async_remote_copy(
            src_ref=normed.at[c],
            dst_ref=heads.at[ctx],
            send_sem=head_send,
            recv_sem=head_recv,
            device_id=(dp, c, tensor),
            device_id_type=MESH,
        )

    now = jnp.zeros((SPAN, SPAN), f32)
    for group in range(n_groups):
        ids = [group * GROUP + b for b in each]
        own[1 + group].wait()
        rest = rows.at[group, pl.ds(0, n_peers - 1)]
        pltpu.make_async_copy(rest, rest, rows_recv.at[group]).wait()
        wide[...] = rows[group].reshape(n_peers * 16, 2 * SPAN).astype(f32)
        got = []
        for c in ids:
            kinds = []
            for offset in (2 * (c % GROUP), 2 * (c % GROUP) + 8):
                even = wide[pl.ds(offset, n_peers, stride=16), :]
                uneven = wide[pl.ds(offset + 1, n_peers, stride=16), :]
                kinds.append(jnp.concatenate([even, uneven], axis=0).T)
            got.append(nn(jnp.concatenate(kinds, axis=0), picks[c]))
        r = [g[:SPAN] for g in got]
        k = [g[SPAN : 2 * SPAN] for g in got]
        v = [g[2 * SPAN : 3 * SPAN] for g in got]
        a = [g[3 * SPAN :] for g in got]
        position = [c * block + lane[0:1] for c in ids]
        start = [doc_start(p) for p in position]
        zeros = jnp.zeros((1, block), jnp.int32)
        start_last = [doc_start(c * block + block - 1 + zeros) for c in ids]
        scaled = [x * gain for x in k]
        unit = [
            x * lax.rsqrt(jnp.sum(x * x, axis=0, keepdims=True) + unit_eps) for x in scaled
        ]
        mixed = [k[i] * (1.0 + (a[i] - 1.0) * mix) for i in each]
        erase = [jnp.where(start[i] == position[i], 0.0, unit[i] * a[i]) for i in each]
        extra = [
            jnp.sum(r[i] * mixed[i] * (bonus + 1.0), axis=0, keepdims=True) * v[i] for i in each
        ]
        recept_up = [r[i] * pre[ids[i], 0] for i in each]
        down = [pre[c, 1] for c in ids]
        unit_up = [unit[i] * pre[ids[i], 2] for i in each]
        opening = [pre[c, 3] for c in ids]
        unit_start = [unit_up[i] * opening[i] for i in each]
        recept_start = [recept_up[i] * opening[i] for i in each]
        erase_down = [(erase[i] * down[i]).T.astype(bf16) for i in each]
        mixed_down = [(mixed[i] * down[i]).T.astype(bf16) for i in each]
        fade = [tips[c, 0:1, :SPAN] for c in ids]
        keep = [tips[c, 0:1, SPAN:] for c in ids]
        scores = [
            nn(
                jnp.concatenate([erase_down[i], mixed_down[i]], axis=0),
                jnp.concatenate([unit_up[i], recept_up[i]], axis=1),
            )
            for i in each
        ]
        inside = [row >= start[i] - ids[i] * block for i in each]
        strict = [inside[i] & (row < lane) for i in each]
        inclusive = [inside[i] & (row <= lane) for i in each]
        erase_mat = [jnp.where(strict[i], scores[i][:block, :block], 0.0) for i in each]
        read_erase = [
            jnp.where(inclusive[i], scores[i][:block, block:], 0.0).astype(bf16) for i in each
        ]
        write_mat = [
            jnp.where(strict[i], scores[i][block:, :block], 0.0).astype(bf16) for i in each
        ]
        read_write = [
            jnp.where(strict[i], scores[i][block:, block:], 0.0).astype(bf16) for i in each
        ]
        power = [jnp.where(nbits[SMALL], -x, 0.0) for x in erase_mat]
        inverse = [eye + x for x in power]
        size = 2
        while size < SMALL:
            power = [nn(x, x) for x in power]
            inverse = [inverse[i] + nn(inverse[i], power[i]) for i in each]
            size *= 2
        size = SMALL
        while size < block:
            ring = nbits[2 * size] & ~nbits[size]
            inner = [nn(jnp.where(ring, erase_mat[i], 0.0), inverse[i]) for i in each]
            inverse = [inverse[i] - nn(inverse[i], inner[i]) for i in each]
            size *= 2
        both = [
            nn(v[i], jnp.concatenate([write_mat[i], read_write[i]], axis=1)) for i in each
        ]
        solved = [
            nn(jnp.concatenate([both[i][:, :block], unit_start[i]], axis=0), inverse[i])
            for i in each
        ]
        read = [nn(solved[i], read_erase[i]) for i in each]
        local_out = [both[i][:, block:] - read[i][:SPAN] + extra[i] for i in each]
        carry_out = [(recept_start[i] - read[i][SPAN:]).astype(bf16) for i in each]
        last = [start[i] == start_last[i] for i in each]
        moved = [nn(jnp.where(last[i], solved[i], 0.0), erase_down[i]) for i in each]
        put = [nn(jnp.where(last[i], v[i], 0.0), mixed_down[i]) for i in each]
        push = [(put[i] - moved[i][:SPAN]) * fade[i] for i in each]
        trans = [(moved[i][SPAN:] * fade[i]).astype(bf16) for i in each]
        whole = []
        for i in each:
            carried = now.astype(bf16)
            whole.append(nn(carried, carry_out[i]) + local_out[i])
            now = now * keep[i] - nn(carried, trans[i]) + push[i]
        for i in each:
            center = whole[i] - jnp.mean(whole[i], axis=0, keepdims=True)
            power2 = jnp.mean(center * center, axis=0, keepdims=True)
            line = (center * lax.rsqrt(power2 + group_eps) * scale + shift).astype(bf16)
            normed[ids[i]] = line

            @pl.when(ctx == ids[i])
            def _(i=i, line=line):
                heads[ids[i]] = line

            @pl.when(ctx != ids[i])
            def _(i=i):
                head_copy(ids[i]).start()

    rest_heads = heads.at[pl.ds(0, n_ctx - 1)]
    pltpu.make_async_copy(rest_heads, rest_heads, head_recv).wait()
    lines = jnp.concatenate(
        [heads[2 * c : 2 * c + 2].reshape(2 * SPAN, block).T for c in range(n_ctx // 2)], axis=1
    )

    def part_copy(n, step):
        other = lax.rem(tensor + step, n_tensor)
        return pltpu.make_async_remote_copy(
            src_ref=parts.at[n, other],
            dst_ref=landed.at[n, step - 1],
            send_sem=part_send.at[n, step - 1],
            recv_sem=part_recv.at[n, step - 1],
            device_id=(dp, ctx, other),
            device_id_type=MESH,
        )

    own_rows = parts.shape[2]
    for n in range(PARTS):
        weight_load(n).wait()
        product = jnp.dot(lines, weight[n], preferred_element_type=f32).astype(bf16)
        for q in range(n_tensor):
            parts[n, q] = product[q * own_rows : (q + 1) * own_rows]
        for step in (2, 1, 3):
            part_copy(n, step).start()
    for n in range(PARTS):
        total = parts[n, tensor].astype(f32)
        for step in range(1, n_tensor):
            part_copy(n, step).wait_recv()
            total = total + landed[n, step - 1].astype(f32)
        out_ref[:, n * width : (n + 1) * width] = total.astype(bf16)
    rest = meta.at[pl.ds(0, n_ctx - 1)]
    pltpu.make_async_copy(rest, rest, note_send).wait()
    for g in range(n_groups):
        rest = rows.at[g, pl.ds(0, n_peers - 1)]
        pltpu.make_async_copy(rest, rest, rows_send.at[g]).wait()
    pltpu.make_async_copy(rest_heads, rest_heads, head_send).wait()
    for n in range(PARTS):
        for step in range(1, n_tensor):
            part_copy(n, step).wait_send()


def hbm():
    return pl.BlockSpec(memory_space=pltpu.HBM)


def local(
    acceptance_vectors,
    lookup_vectors,
    payload_vectors,
    incontext_adaptation,
    fading_codes,
    stacked_line_pointer,
    article_extents,
    feature_fading,
    erasure_lookup_scaling,
    lookup_mixture_share,
    reward_coefficients,
    cluster_standard_scaling,
    cluster_standard_offset,
    final_projection,
):
    tokens, features = acceptance_vectors.shape
    columns = final_projection.shape[1]
    n_dp = lax.axis_size("dp")
    n_ctx = lax.axis_size("context")
    n_tensor = lax.axis_size("tensor")
    n_peers = n_dp * n_ctx
    n_groups = n_ctx // GROUP
    own_rows = tokens // n_tensor
    width = columns // PARTS
    vectors = [
        item.reshape(features // 128, 128)
        for item in (
            feature_fading,
            erasure_lookup_scaling,
            lookup_mixture_share,
            reward_coefficients,
            cluster_standard_scaling,
            cluster_standard_offset,
        )
    ]
    dma = pltpu.SemaphoreType.DMA
    vm = pltpu.VMEM
    summed = pl.pallas_call(
        functools.partial(layer, n_dp, n_ctx, n_tensor),
        out_shape=jax.ShapeDtypeStruct((own_rows, columns), bf16),
        in_specs=[hbm()] * 14,
        out_specs=pl.BlockSpec(memory_space=pltpu.VMEM),
        scratch_shapes=[
            vm((tokens, features), bf16),
            vm((tokens, features), bf16),
            vm((tokens, features), bf16),
            vm((tokens, features), bf16),
            vm((n_ctx, tokens), jnp.int32),
            vm((1, tokens), jnp.int32),
            vm((1, article_extents.shape[1]), jnp.int32),
            vm((6, features // 128, 128), f32),
            vm((PARTS, features, width), bf16),
            vm((n_groups, n_peers, 16, 2 * SPAN), bf16),
            vm((n_groups, n_peers, 16, 2 * SPAN), bf16),
            vm((n_peers * 16, 2 * SPAN), f32),
            vm((n_ctx, 8, tokens), f32),
            vm((n_ctx, 8, tokens), f32),
            vm((n_ctx, 4, SPAN, tokens), f32),
            vm((n_ctx, 8, tokens), f32),
            vm((n_ctx, tokens, tokens), bf16),
            vm((n_ctx, SPAN, tokens), bf16),
            vm((n_ctx, SPAN, tokens), bf16),
            vm((PARTS, n_tensor, own_rows, width), bf16),
            vm((PARTS, n_tensor - 1, own_rows, width), bf16),
            dma((13,)),
            dma((PARTS,)),
            dma((n_groups + 1,)),
            dma,
            dma,
            dma((n_groups,)),
            dma((n_groups,)),
            dma,
            dma,
            dma((PARTS, n_tensor - 1)),
            dma((PARTS, n_tensor - 1)),
        ],
        compiler_params=pltpu.CompilerParams(
            collective_id=0, has_side_effects=True, vmem_limit_bytes=52 << 20
        ),
    )(
        acceptance_vectors,
        lookup_vectors,
        payload_vectors,
        incontext_adaptation,
        fading_codes[0].T,
        stacked_line_pointer,
        article_extents,
        *vectors,
        final_projection,
    )
    return summed.reshape(1, own_rows, columns)


def solution(mesh):
    return jax.shard_map(
        local,
        mesh=mesh,
        in_specs=(
            P(("dp", "context"), "tensor"),
            P(("dp", "context"), "tensor"),
            P(("dp", "context"), "tensor"),
            P(("dp", "context"), "tensor"),
            P("dp", "context", "tensor"),
            P("dp", "context"),
            P("dp", None),
            P("tensor"),
            P("tensor"),
            P("tensor"),
            P("tensor"),
            P("tensor"),
            P("tensor"),
            P("tensor", None),
        ),
        out_specs=P("dp", ("context", "tensor"), None),
        check_vma=False,
    )
```

```python
import functools

import jax
import jax.numpy as jnp
from jax import lax
from jax.experimental import pallas as pl
from jax.experimental.pallas import tpu as pltpu
from jax.sharding import PartitionSpec as P

MESH = pl.DeviceIdType.MESH
SPAN = 64
GROUP = 4
SMALL = 8
PARTS = 4
decay_cap = 0.606531
unit_eps = 1e-06
group_eps = 0.00064
f32 = jnp.float32
bf16 = jnp.bfloat16


def nn(a, b):
    return lax.dot_general(
        a.astype(bf16), b.astype(bf16), (((1,), (0,)), ((), ())), preferred_element_type=f32
    )


def layer(
    n_dp,
    n_ctx,
    n_tensor,
    r_hbm,
    k_hbm,
    v_hbm,
    a_hbm,
    code_hbm,
    ptr_hbm,
    lens_hbm,
    rate_hbm,
    gain_hbm,
    mix_hbm,
    bonus_hbm,
    scale_hbm,
    shift_hbm,
    weight_hbm,
    out_ref,
    r_ref,
    k_ref,
    v_ref,
    a_ref,
    code_ref,
    ptr_ref,
    lens_ref,
    lines_ref,
    weight,
    packed,
    rows,
    wide,
    notes,
    meta,
    pre,
    tips,
    picks,
    normed,
    heads,
    parts,
    landed,
    load_sem,
    weight_sem,
    own_sem,
    note_send,
    note_recv,
    rows_send,
    rows_recv,
    head_send,
    head_recv,
    part_send,
    part_recv,
):
    dp = lax.axis_index("dp")
    ctx = lax.axis_index("context")
    tensor = lax.axis_index("tensor")
    n_peers = n_dp * n_ctx
    me = dp * n_ctx + ctx
    block = r_ref.shape[0]
    n_groups = n_ctx // GROUP
    width = weight.shape[2]

    def place(index):
        return (index // n_ctx, lax.rem(index, n_ctx), tensor)

    barrier = pltpu.get_barrier_semaphore()

    def greet(step, carry):
        other = lax.rem(me + step, n_peers)
        pl.semaphore_signal(barrier, inc=1, device_id=place(other), device_id_type=MESH)
        return carry

    lax.fori_loop(1, n_peers, greet, 0)
    for step in range(1, n_tensor):
        other = lax.rem(tensor + step, n_tensor)
        pl.semaphore_signal(barrier, inc=1, device_id=(dp, ctx, other), device_id_type=MESH)

    loads = [
        (r_hbm, r_ref),
        (k_hbm, k_ref),
        (v_hbm, v_ref),
        (a_hbm, a_ref),
        (code_hbm, code_ref),
        (ptr_hbm, ptr_ref),
        (lens_hbm, lens_ref),
    ]
    for i, ref in enumerate((rate_hbm, gain_hbm, mix_hbm, bonus_hbm, scale_hbm, shift_hbm)):
        loads.append((ref, lines_ref.at[i]))
    loads = [
        pltpu.make_async_copy(src, dst, load_sem.at[i]) for i, (src, dst) in enumerate(loads)
    ]
    for load in loads:
        load.start()

    def weight_load(n):
        return pltpu.make_async_copy(
            weight_hbm.at[:, pl.ds(n * width, width)], weight.at[n], weight_sem.at[n]
        )

    for load in loads:
        load.wait()
    for n in range(PARTS):
        weight_load(n).start()

    per_seq = block // n_dp
    for pair in range(n_ctx // 2):
        lanes = slice(128 * pair, 128 * pair + 128)
        r, k, v, a = r_ref[:, lanes], k_ref[:, lanes], v_ref[:, lanes], a_ref[:, lanes]
        for half, part in ((0, slice(0, SPAN)), (1, slice(SPAN, 128))):
            rk = jnp.concatenate([r[:, part], k[:, part]], axis=1).astype(f32)
            va = jnp.concatenate([v[:, part], a[:, part]], axis=1).astype(f32)
            for s in range(n_dp):
                slot = s * n_ctx + 2 * pair + half
                for g in range(n_groups):
                    piece = slice(s * per_seq + 8 * g, s * per_seq + 8 * g + 8)
                    packed[g, slot] = jnp.concatenate([rk[piece], va[piece]], axis=0).astype(bf16)
    codes = code_ref[...].astype(f32)
    pointers = ptr_ref[...].astype(f32)
    for c in range(n_ctx):
        notes[c] = jnp.concatenate(
            [pointers, codes[c : c + 1, :], jnp.zeros((6, block), f32)], axis=0
        )

    pl.semaphore_wait(barrier, n_peers - 1 + n_tensor - 1)

    own = [pltpu.make_async_copy(notes.at[ctx], meta.at[ctx], own_sem.at[n_groups])]
    for g in range(n_groups):
        own.append(pltpu.make_async_copy(packed.at[g, me], rows.at[g, me], own_sem.at[g]))
    for copy in own:
        copy.start()

    def send_note(step, carry):
        other = lax.rem(ctx + step, n_ctx)
        pltpu.make_async_remote_copy(
            src_ref=notes.at[other],
            dst_ref=meta.at[ctx],
            send_sem=note_send,
            recv_sem=note_recv,
            device_id=(dp, other, tensor),
            device_id_type=MESH,
        ).start()
        return carry

    lax.fori_loop(1, n_ctx, send_note, 0)
    for g in range(n_groups):

        def send_rows(step, carry, g=g):
            other = lax.rem(me + step, n_peers)
            pltpu.make_async_remote_copy(
                src_ref=packed.at[g, other],
                dst_ref=rows.at[g, me],
                send_sem=rows_send.at[g],
                recv_sem=rows_recv.at[g],
                device_id=place(other),
                device_id_type=MESH,
            ).start()
            return carry

        lax.fori_loop(1, n_peers, send_rows, 0)

    odd = lax.rem(ctx, 2) == 1
    lane = lax.broadcasted_iota(jnp.int32, (block, block), 1)
    row = lax.broadcasted_iota(jnp.int32, (block, block), 0)
    flip = (lane[:SPAN] & (SPAN - 1)) == row[:SPAN]

    def column(index):
        line = lines_ref[index, pl.ds(ctx // 2, 1), :]
        line = jnp.where(odd, line[:, SPAN:], line[:, :SPAN])
        line = jnp.broadcast_to(line, (SPAN, SPAN))
        return jnp.sum(jnp.where(flip[:, :SPAN], line, 0.0), axis=1, keepdims=True) + jnp.zeros(
            (SPAN, block), f32
        )

    rate, gain, mix, bonus, scale, shift = [column(index) for index in range(6)]
    lens = lens_ref[...]
    first = lens[:, 0:1]
    second = first + lens[:, 1:2]
    third = second + lens[:, 2:3]

    def doc_start(position):
        found = jnp.where(position >= first, first, 0)
        found = jnp.where(position >= second, second, found)
        return jnp.where(position >= third, third, found)

    mid = block // 2
    sums = jnp.concatenate(
        [
            (row <= lane).astype(f32) - (row < mid).astype(f32),
            (row >= mid).astype(f32),
            (row < mid).astype(f32),
        ],
        axis=1,
    ).astype(bf16)
    eye = (row == lane).astype(f32)
    nbits = {}
    size = SMALL
    while size <= block:
        nbits[size] = (row // size) == (lane // size)
        size *= 2
    own[0].wait()
    rest = meta.at[pl.ds(0, n_ctx - 1)]
    pltpu.make_async_copy(rest, rest, note_recv).wait()
    each = range(GROUP)
    for group in range(n_groups):
        ids = [group * GROUP + b for b in each]
        decay = [-decay_cap * (1.0 - jnp.exp(-rate * meta[c, 1:2, :])) for c in ids]
        cums = []
        for d in decay:
            d0 = d.astype(bf16)
            left = d - d0.astype(f32)
            d1 = left.astype(bf16)
            d2 = (left - d1.astype(f32)).astype(bf16)
            total = nn(jnp.concatenate([d0, d1, d2], axis=0), sums)
            cums.append(total[:SPAN] + total[SPAN : 2 * SPAN] + total[2 * SPAN :])
        for i, c in enumerate(ids):
            position = c * block + lane[0:1]
            start = doc_start(position)
            about = cums[i][:, :block]
            to_end = cums[i][:, block : 2 * block]
            to_mid = cums[i][:, 2 * block :]
            pre[c, 0] = jnp.exp(about)
            pre[c, 1] = jnp.exp(-about)
            pre[c, 2] = jnp.exp(about - decay[i])
            pre[c, 3] = jnp.where(start < c * block, jnp.exp(to_mid), 0.0)
            choice = jnp.where(lane[:SPAN] < SPAN, to_end, to_end + to_mid)
            ends = jnp.exp(jnp.sum(jnp.where(flip, choice, 0.0), axis=0, keepdims=True))
            through = doc_start(c * block + block - 1 + jnp.zeros((1, block), jnp.int32)) < c * block
            ends = jnp.where(through | (lane[0:1] < SPAN), ends, 0.0)
            tips[c] = jnp.broadcast_to(ends, (8, block))
            pointer = meta[c, 0:1, :].astype(jnp.int32)
            where = (pointer & 1) * n_peers + (pointer // block)
            picks[c] = (row == where).astype(bf16)

    def head_copy(c):
        return pltpu.make_async_remote_copy(
            src_ref=normed.at[c],
            dst_ref=heads.at[ctx],
            send_sem=head_send,
            recv_sem=head_recv,
            device_id=(dp, c, tensor),
            device_id_type=MESH,
        )

    now = jnp.zeros((SPAN, SPAN), f32)
    for group in range(n_groups):
        ids = [group * GROUP + b for b in each]
        own[1 + group].wait()
        rest = rows.at[group, pl.ds(0, n_peers - 1)]
        pltpu.make_async_copy(rest, rest, rows_recv.at[group]).wait()
        wide[...] = rows[group].reshape(n_peers * 16, 2 * SPAN).astype(f32)
        got = []
        for c in ids:
            kinds = []
            for offset in (2 * (c % GROUP), 2 * (c % GROUP) + 8):
                even = wide[pl.ds(offset, n_peers, stride=16), :]
                uneven = wide[pl.ds(offset + 1, n_peers, stride=16), :]
                kinds.append(jnp.concatenate([even, uneven], axis=0).T)
            got.append(nn(jnp.concatenate(kinds, axis=0), picks[c]))
        r = [g[:SPAN] for g in got]
        k = [g[SPAN : 2 * SPAN] for g in got]
        v = [g[2 * SPAN : 3 * SPAN] for g in got]
        a = [g[3 * SPAN :] for g in got]
        position = [c * block + lane[0:1] for c in ids]
        start = [doc_start(p) for p in position]
        zeros = jnp.zeros((1, block), jnp.int32)
        start_last = [doc_start(c * block + block - 1 + zeros) for c in ids]
        scaled = [x * gain for x in k]
        unit = [
            x * lax.rsqrt(jnp.sum(x * x, axis=0, keepdims=True) + unit_eps) for x in scaled
        ]
        mixed = [k[i] * (1.0 + (a[i] - 1.0) * mix) for i in each]
        erase = [jnp.where(start[i] == position[i], 0.0, unit[i] * a[i]) for i in each]
        extra = [
            jnp.sum(r[i] * mixed[i] * (bonus + 1.0), axis=0, keepdims=True) * v[i] for i in each
        ]
        recept_up = [r[i] * pre[ids[i], 0] for i in each]
        down = [pre[c, 1] for c in ids]
        unit_up = [unit[i] * pre[ids[i], 2] for i in each]
        opening = [pre[c, 3] for c in ids]
        unit_start = [unit_up[i] * opening[i] for i in each]
        recept_start = [recept_up[i] * opening[i] for i in each]
        erase_down = [(erase[i] * down[i]).T.astype(bf16) for i in each]
        mixed_down = [(mixed[i] * down[i]).T.astype(bf16) for i in each]
        fade = [tips[c, 0:1, :SPAN] for c in ids]
        keep = [tips[c, 0:1, SPAN:] for c in ids]
        scores = [
            nn(
                jnp.concatenate([erase_down[i], mixed_down[i]], axis=0),
                jnp.concatenate([unit_up[i], recept_up[i]], axis=1),
            )
            for i in each
        ]
        inside = [row >= start[i] - ids[i] * block for i in each]
        strict = [inside[i] & (row < lane) for i in each]
        inclusive = [inside[i] & (row <= lane) for i in each]
        erase_mat = [jnp.where(strict[i], scores[i][:block, :block], 0.0) for i in each]
        read_erase = [
            jnp.where(inclusive[i], scores[i][:block, block:], 0.0).astype(bf16) for i in each
        ]
        write_mat = [
            jnp.where(strict[i], scores[i][block:, :block], 0.0).astype(bf16) for i in each
        ]
        read_write = [
            jnp.where(strict[i], scores[i][block:, block:], 0.0).astype(bf16) for i in each
        ]
        power = [jnp.where(nbits[SMALL], -x, 0.0) for x in erase_mat]
        inverse = [eye + x for x in power]
        size = 2
        while size < SMALL:
            power = [nn(x, x) for x in power]
            inverse = [inverse[i] + nn(inverse[i], power[i]) for i in each]
            size *= 2
        size = SMALL
        while size < block:
            ring = nbits[2 * size] & ~nbits[size]
            inner = [nn(jnp.where(ring, erase_mat[i], 0.0), inverse[i]) for i in each]
            inverse = [inverse[i] - nn(inverse[i], inner[i]) for i in each]
            size *= 2
        both = [
            nn(v[i], jnp.concatenate([write_mat[i], read_write[i]], axis=1)) for i in each
        ]
        solved = [
            nn(jnp.concatenate([both[i][:, :block], unit_start[i]], axis=0), inverse[i])
            for i in each
        ]
        read = [nn(solved[i], read_erase[i]) for i in each]
        local_out = [both[i][:, block:] - read[i][:SPAN] + extra[i] for i in each]
        carry_out = [(recept_start[i] - read[i][SPAN:]).astype(bf16) for i in each]
        last = [start[i] == start_last[i] for i in each]
        moved = [nn(jnp.where(last[i], solved[i], 0.0), erase_down[i]) for i in each]
        put = [nn(jnp.where(last[i], v[i], 0.0), mixed_down[i]) for i in each]
        push = [(put[i] - moved[i][:SPAN]) * fade[i] for i in each]
        trans = [(moved[i][SPAN:] * fade[i]).astype(bf16) for i in each]
        whole = []
        for i in each:
            carried = now.astype(bf16)
            whole.append(nn(carried, carry_out[i]) + local_out[i])
            now = now * keep[i] - nn(carried, trans[i]) + push[i]
        for i in each:
            center = whole[i] - jnp.mean(whole[i], axis=0, keepdims=True)
            power2 = jnp.mean(center * center, axis=0, keepdims=True)
            line = (center * lax.rsqrt(power2 + group_eps) * scale + shift).astype(bf16)
            normed[ids[i]] = line

            @pl.when(ctx == ids[i])
            def _(i=i, line=line):
                heads[ids[i]] = line

            @pl.when(ctx != ids[i])
            def _(i=i):
                head_copy(ids[i]).start()

    rest_heads = heads.at[pl.ds(0, n_ctx - 1)]
    pltpu.make_async_copy(rest_heads, rest_heads, head_recv).wait()
    lines = jnp.concatenate(
        [heads[2 * c : 2 * c + 2].reshape(2 * SPAN, block).T for c in range(n_ctx // 2)], axis=1
    )

    def part_copy(n, step):
        other = lax.rem(tensor + step, n_tensor)
        return pltpu.make_async_remote_copy(
            src_ref=parts.at[n, other],
            dst_ref=landed.at[n, step - 1],
            send_sem=part_send.at[n, step - 1],
            recv_sem=part_recv.at[n, step - 1],
            device_id=(dp, ctx, other),
            device_id_type=MESH,
        )

    own_rows = parts.shape[2]
    for n in range(PARTS):
        weight_load(n).wait()
        product = jnp.dot(lines, weight[n], preferred_element_type=f32).astype(bf16)
        for q in range(n_tensor):
            parts[n, q] = product[q * own_rows : (q + 1) * own_rows]
        for step in (2, 1, 3):
            part_copy(n, step).start()
    for n in range(PARTS):
        total = parts[n, tensor].astype(f32)
        for step in range(1, n_tensor):
            part_copy(n, step).wait_recv()
            total = total + landed[n, step - 1].astype(f32)
        out_ref[:, n * width : (n + 1) * width] = total.astype(bf16)
    rest = meta.at[pl.ds(0, n_ctx - 1)]
    pltpu.make_async_copy(rest, rest, note_send).wait()
    for g in range(n_groups):
        rest = rows.at[g, pl.ds(0, n_peers - 1)]
        pltpu.make_async_copy(rest, rest, rows_send.at[g]).wait()
    pltpu.make_async_copy(rest_heads, rest_heads, head_send).wait()
    for n in range(PARTS):
        for step in range(1, n_tensor):
            part_copy(n, step).wait_send()


def hbm():
    return pl.BlockSpec(memory_space=pltpu.HBM)


def local(
    acceptance_vectors,
    lookup_vectors,
    payload_vectors,
    incontext_adaptation,
    fading_codes,
    stacked_line_pointer,
    article_extents,
    feature_fading,
    erasure_lookup_scaling,
    lookup_mixture_share,
    reward_coefficients,
    cluster_standard_scaling,
    cluster_standard_offset,
    final_projection,
):
    tokens, features = acceptance_vectors.shape
    columns = final_projection.shape[1]
    n_dp = lax.axis_size("dp")
    n_ctx = lax.axis_size("context")
    n_tensor = lax.axis_size("tensor")
    n_peers = n_dp * n_ctx
    n_groups = n_ctx // GROUP
    own_rows = tokens // n_tensor
    width = columns // PARTS
    vectors = [
        item.reshape(features // 128, 128)
        for item in (
            feature_fading,
            erasure_lookup_scaling,
            lookup_mixture_share,
            reward_coefficients,
            cluster_standard_scaling,
            cluster_standard_offset,
        )
    ]
    dma = pltpu.SemaphoreType.DMA
    vm = pltpu.VMEM
    summed = pl.pallas_call(
        functools.partial(layer, n_dp, n_ctx, n_tensor),
        out_shape=jax.ShapeDtypeStruct((own_rows, columns), bf16),
        in_specs=[hbm()] * 14,
        out_specs=pl.BlockSpec(memory_space=pltpu.VMEM),
        scratch_shapes=[
            vm((tokens, features), bf16),
            vm((tokens, features), bf16),
            vm((tokens, features), bf16),
            vm((tokens, features), bf16),
            vm((n_ctx, tokens), jnp.int32),
            vm((1, tokens), jnp.int32),
            vm((1, article_extents.shape[1]), jnp.int32),
            vm((6, features // 128, 128), f32),
            vm((PARTS, features, width), bf16),
            vm((n_groups, n_peers, 16, 2 * SPAN), bf16),
            vm((n_groups, n_peers, 16, 2 * SPAN), bf16),
            vm((n_peers * 16, 2 * SPAN), f32),
            vm((n_ctx, 8, tokens), f32),
            vm((n_ctx, 8, tokens), f32),
            vm((n_ctx, 4, SPAN, tokens), f32),
            vm((n_ctx, 8, tokens), f32),
            vm((n_ctx, tokens, tokens), bf16),
            vm((n_ctx, SPAN, tokens), bf16),
            vm((n_ctx, SPAN, tokens), bf16),
            vm((PARTS, n_tensor, own_rows, width), bf16),
            vm((PARTS, n_tensor - 1, own_rows, width), bf16),
            dma((13,)),
            dma((PARTS,)),
            dma((n_groups + 1,)),
            dma,
            dma,
            dma((n_groups,)),
            dma((n_groups,)),
            dma,
            dma,
            dma((PARTS, n_tensor - 1)),
            dma((PARTS, n_tensor - 1)),
        ],
        compiler_params=pltpu.CompilerParams(
            collective_id=0, has_side_effects=True, vmem_limit_bytes=60 << 20
        ),
    )(
        acceptance_vectors,
        lookup_vectors,
        payload_vectors,
        incontext_adaptation,
        fading_codes[0].T,
        stacked_line_pointer,
        article_extents,
        *vectors,
        final_projection,
    )
    return summed.reshape(1, own_rows, columns)


def solution(mesh):
    return jax.shard_map(
        local,
        mesh=mesh,
        in_specs=(
            P(("dp", "context"), "tensor"),
            P(("dp", "context"), "tensor"),
            P(("dp", "context"), "tensor"),
            P(("dp", "context"), "tensor"),
            P("dp", "context", "tensor"),
            P("dp", "context"),
            P("dp", None),
            P("tensor"),
            P("tensor"),
            P("tensor"),
            P("tensor"),
            P("tensor"),
            P("tensor"),
            P("tensor", None),
        ),
        out_specs=P("dp", ("context", "tensor"), None),
        check_vma=False,
    )
```

```python
import functools

import jax
import jax.numpy as jnp
from jax import lax
from jax.experimental import pallas as pl
from jax.experimental.pallas import tpu as pltpu
from jax.sharding import PartitionSpec as P

MESH = pl.DeviceIdType.MESH
SPAN = 64
GROUP = 4
SMALL = 8
PARTS = 8
LAG = 6
decay_cap = 0.606531
unit_eps = 1e-06
group_eps = 0.00064
f32 = jnp.float32
bf16 = jnp.bfloat16


def nn(a, b):
    return lax.dot_general(
        a.astype(bf16), b.astype(bf16), (((1,), (0,)), ((), ())), preferred_element_type=f32
    )


def layer(
    n_dp,
    n_ctx,
    n_tensor,
    r_hbm,
    k_hbm,
    v_hbm,
    a_hbm,
    code_hbm,
    ptr_hbm,
    lens_hbm,
    rate_hbm,
    gain_hbm,
    mix_hbm,
    bonus_hbm,
    scale_hbm,
    shift_hbm,
    weight_hbm,
    out_ref,
    r_ref,
    k_ref,
    v_ref,
    a_ref,
    code_ref,
    ptr_ref,
    lens_ref,
    lines_ref,
    weight,
    packed,
    rows,
    wide,
    notes,
    meta,
    pre,
    tips,
    picks,
    normed,
    heads,
    parts,
    relay_in,
    relay_out,
    landed,
    load_sem,
    weight_sem,
    own_sem,
    note_send,
    note_recv,
    rows_send,
    rows_recv,
    head_send,
    head_recv,
    part_send,
    part_recv,
):
    dp = lax.axis_index("dp")
    ctx = lax.axis_index("context")
    tensor = lax.axis_index("tensor")
    n_peers = n_dp * n_ctx
    me = dp * n_ctx + ctx
    block = r_ref.shape[0]
    n_groups = n_ctx // GROUP
    width = weight.shape[2]

    def place(index):
        return (index // n_ctx, lax.rem(index, n_ctx), tensor)

    barrier = pltpu.get_barrier_semaphore()

    def greet(step, carry):
        other = lax.rem(me + step, n_peers)
        pl.semaphore_signal(barrier, inc=1, device_id=place(other), device_id_type=MESH)
        return carry

    lax.fori_loop(1, n_peers, greet, 0)
    for step in range(1, n_tensor):
        other = lax.rem(tensor + step, n_tensor)
        pl.semaphore_signal(barrier, inc=1, device_id=(dp, ctx, other), device_id_type=MESH)

    loads = [
        (r_hbm, r_ref),
        (k_hbm, k_ref),
        (v_hbm, v_ref),
        (a_hbm, a_ref),
        (code_hbm, code_ref),
        (ptr_hbm, ptr_ref),
        (lens_hbm, lens_ref),
    ]
    for i, ref in enumerate((rate_hbm, gain_hbm, mix_hbm, bonus_hbm, scale_hbm, shift_hbm)):
        loads.append((ref, lines_ref.at[i]))
    loads = [
        pltpu.make_async_copy(src, dst, load_sem.at[i]) for i, (src, dst) in enumerate(loads)
    ]
    for load in loads:
        load.start()

    def weight_load(n):
        return pltpu.make_async_copy(
            weight_hbm.at[:, pl.ds(n * width, width)], weight.at[n], weight_sem.at[n]
        )

    for load in loads:
        load.wait()
    for n in range(PARTS):
        weight_load(n).start()

    per_seq = block // n_dp
    for pair in range(n_ctx // 2):
        lanes = slice(128 * pair, 128 * pair + 128)
        r, k, v, a = r_ref[:, lanes], k_ref[:, lanes], v_ref[:, lanes], a_ref[:, lanes]
        for half, part in ((0, slice(0, SPAN)), (1, slice(SPAN, 128))):
            rk = jnp.concatenate([r[:, part], k[:, part]], axis=1).astype(f32)
            va = jnp.concatenate([v[:, part], a[:, part]], axis=1).astype(f32)
            for s in range(n_dp):
                slot = s * n_ctx + 2 * pair + half
                for g in range(n_groups):
                    piece = slice(s * per_seq + 8 * g, s * per_seq + 8 * g + 8)
                    packed[g, slot] = jnp.concatenate([rk[piece], va[piece]], axis=0).astype(bf16)
    codes = code_ref[...].astype(f32)
    pointers = ptr_ref[...].astype(f32)
    for c in range(n_ctx):
        notes[c] = jnp.concatenate(
            [pointers, codes[c : c + 1, :], jnp.zeros((6, block), f32)], axis=0
        )

    pl.semaphore_wait(barrier, n_peers - 1 + n_tensor - 1)

    own = [pltpu.make_async_copy(notes.at[ctx], meta.at[ctx], own_sem.at[n_groups])]
    for g in range(n_groups):
        own.append(pltpu.make_async_copy(packed.at[g, me], rows.at[g, me], own_sem.at[g]))
    for copy in own:
        copy.start()

    def send_note(step, carry):
        other = lax.rem(ctx + step, n_ctx)
        pltpu.make_async_remote_copy(
            src_ref=notes.at[other],
            dst_ref=meta.at[ctx],
            send_sem=note_send,
            recv_sem=note_recv,
            device_id=(dp, other, tensor),
            device_id_type=MESH,
        ).start()
        return carry

    lax.fori_loop(1, n_ctx, send_note, 0)
    for g in range(n_groups):

        def send_rows(step, carry, g=g):
            other = lax.rem(me + step, n_peers)
            pltpu.make_async_remote_copy(
                src_ref=packed.at[g, other],
                dst_ref=rows.at[g, me],
                send_sem=rows_send.at[g],
                recv_sem=rows_recv.at[g],
                device_id=place(other),
                device_id_type=MESH,
            ).start()
            return carry

        lax.fori_loop(1, n_peers, send_rows, 0)

    odd = lax.rem(ctx, 2) == 1
    lane = lax.broadcasted_iota(jnp.int32, (block, block), 1)
    row = lax.broadcasted_iota(jnp.int32, (block, block), 0)
    flip = (lane[:SPAN] & (SPAN - 1)) == row[:SPAN]

    def column(index):
        line = lines_ref[index, pl.ds(ctx // 2, 1), :]
        line = jnp.where(odd, line[:, SPAN:], line[:, :SPAN])
        line = jnp.broadcast_to(line, (SPAN, SPAN))
        return jnp.sum(jnp.where(flip[:, :SPAN], line, 0.0), axis=1, keepdims=True) + jnp.zeros(
            (SPAN, block), f32
        )

    rate, gain, mix, bonus, scale, shift = [column(index) for index in range(6)]
    lens = lens_ref[...]
    first = lens[:, 0:1]
    second = first + lens[:, 1:2]
    third = second + lens[:, 2:3]

    def doc_start(position):
        found = jnp.where(position >= first, first, 0)
        found = jnp.where(position >= second, second, found)
        return jnp.where(position >= third, third, found)

    mid = block // 2
    sums = jnp.concatenate(
        [
            (row <= lane).astype(f32) - (row < mid).astype(f32),
            (row >= mid).astype(f32),
            (row < mid).astype(f32),
        ],
        axis=1,
    ).astype(bf16)
    eye = (row == lane).astype(f32)
    nbits = {}
    size = SMALL
    while size <= block:
        nbits[size] = (row // size) == (lane // size)
        size *= 2
    own[0].wait()
    rest = meta.at[pl.ds(0, n_ctx - 1)]
    pltpu.make_async_copy(rest, rest, note_recv).wait()
    each = range(GROUP)
    for group in range(n_groups):
        ids = [group * GROUP + b for b in each]
        decay = [-decay_cap * (1.0 - jnp.exp(-rate * meta[c, 1:2, :])) for c in ids]
        cums = []
        for d in decay:
            d0 = d.astype(bf16)
            left = d - d0.astype(f32)
            d1 = left.astype(bf16)
            d2 = (left - d1.astype(f32)).astype(bf16)
            total = nn(jnp.concatenate([d0, d1, d2], axis=0), sums)
            cums.append(total[:SPAN] + total[SPAN : 2 * SPAN] + total[2 * SPAN :])
        for i, c in enumerate(ids):
            position = c * block + lane[0:1]
            start = doc_start(position)
            about = cums[i][:, :block]
            to_end = cums[i][:, block : 2 * block]
            to_mid = cums[i][:, 2 * block :]
            pre[c, 0] = jnp.exp(about)
            pre[c, 1] = jnp.exp(-about)
            pre[c, 2] = jnp.exp(about - decay[i])
            pre[c, 3] = jnp.where(start < c * block, jnp.exp(to_mid), 0.0)
            choice = jnp.where(lane[:SPAN] < SPAN, to_end, to_end + to_mid)
            ends = jnp.exp(jnp.sum(jnp.where(flip, choice, 0.0), axis=0, keepdims=True))
            through = doc_start(c * block + block - 1 + jnp.zeros((1, block), jnp.int32)) < c * block
            ends = jnp.where(through | (lane[0:1] < SPAN), ends, 0.0)
            tips[c] = jnp.broadcast_to(ends, (8, block))
            pointer = meta[c, 0:1, :].astype(jnp.int32)
            where = (pointer & 1) * n_peers + (pointer // block)
            picks[c] = (row == where).astype(bf16)

    def head_copy(c):
        return pltpu.make_async_remote_copy(
            src_ref=normed.at[c],
            dst_ref=heads.at[ctx],
            send_sem=head_send,
            recv_sem=head_recv,
            device_id=(dp, c, tensor),
            device_id_type=MESH,
        )

    now = jnp.zeros((SPAN, SPAN), f32)
    for group in range(n_groups):
        ids = [group * GROUP + b for b in each]
        own[1 + group].wait()
        rest = rows.at[group, pl.ds(0, n_peers - 1)]
        pltpu.make_async_copy(rest, rest, rows_recv.at[group]).wait()
        wide[...] = rows[group].reshape(n_peers * 16, 2 * SPAN).astype(f32)
        got = []
        for c in ids:
            kinds = []
            for offset in (2 * (c % GROUP), 2 * (c % GROUP) + 8):
                even = wide[pl.ds(offset, n_peers, stride=16), :]
                uneven = wide[pl.ds(offset + 1, n_peers, stride=16), :]
                kinds.append(jnp.concatenate([even, uneven], axis=0).T)
            got.append(nn(jnp.concatenate(kinds, axis=0), picks[c]))
        r = [g[:SPAN] for g in got]
        k = [g[SPAN : 2 * SPAN] for g in got]
        v = [g[2 * SPAN : 3 * SPAN] for g in got]
        a = [g[3 * SPAN :] for g in got]
        position = [c * block + lane[0:1] for c in ids]
        start = [doc_start(p) for p in position]
        zeros = jnp.zeros((1, block), jnp.int32)
        start_last = [doc_start(c * block + block - 1 + zeros) for c in ids]
        scaled = [x * gain for x in k]
        unit = [
            x * lax.rsqrt(jnp.sum(x * x, axis=0, keepdims=True) + unit_eps) for x in scaled
        ]
        mixed = [k[i] * (1.0 + (a[i] - 1.0) * mix) for i in each]
        erase = [jnp.where(start[i] == position[i], 0.0, unit[i] * a[i]) for i in each]
        extra = [
            jnp.sum(r[i] * mixed[i] * (bonus + 1.0), axis=0, keepdims=True) * v[i] for i in each
        ]
        recept_up = [r[i] * pre[ids[i], 0] for i in each]
        down = [pre[c, 1] for c in ids]
        unit_up = [unit[i] * pre[ids[i], 2] for i in each]
        opening = [pre[c, 3] for c in ids]
        unit_start = [unit_up[i] * opening[i] for i in each]
        recept_start = [recept_up[i] * opening[i] for i in each]
        erase_down = [(erase[i] * down[i]).T.astype(bf16) for i in each]
        mixed_down = [(mixed[i] * down[i]).T.astype(bf16) for i in each]
        fade = [tips[c, 0:1, :SPAN] for c in ids]
        keep = [tips[c, 0:1, SPAN:] for c in ids]
        scores = [
            nn(
                jnp.concatenate([erase_down[i], mixed_down[i]], axis=0),
                jnp.concatenate([unit_up[i], recept_up[i]], axis=1),
            )
            for i in each
        ]
        inside = [row >= start[i] - ids[i] * block for i in each]
        strict = [inside[i] & (row < lane) for i in each]
        inclusive = [inside[i] & (row <= lane) for i in each]
        erase_mat = [jnp.where(strict[i], scores[i][:block, :block], 0.0) for i in each]
        read_erase = [
            jnp.where(inclusive[i], scores[i][:block, block:], 0.0).astype(bf16) for i in each
        ]
        write_mat = [
            jnp.where(strict[i], scores[i][block:, :block], 0.0).astype(bf16) for i in each
        ]
        read_write = [
            jnp.where(strict[i], scores[i][block:, block:], 0.0).astype(bf16) for i in each
        ]
        power = [jnp.where(nbits[SMALL], -x, 0.0) for x in erase_mat]
        inverse = [eye + x for x in power]
        size = 2
        while size < SMALL:
            power = [nn(x, x) for x in power]
            inverse = [inverse[i] + nn(inverse[i], power[i]) for i in each]
            size *= 2
        size = SMALL
        while size < block:
            ring = nbits[2 * size] & ~nbits[size]
            inner = [nn(jnp.where(ring, erase_mat[i], 0.0), inverse[i]) for i in each]
            inverse = [inverse[i] - nn(inverse[i], inner[i]) for i in each]
            size *= 2
        both = [
            nn(v[i], jnp.concatenate([write_mat[i], read_write[i]], axis=1)) for i in each
        ]
        solved = [
            nn(jnp.concatenate([both[i][:, :block], unit_start[i]], axis=0), inverse[i])
            for i in each
        ]
        read = [nn(solved[i], read_erase[i]) for i in each]
        local_out = [both[i][:, block:] - read[i][:SPAN] + extra[i] for i in each]
        carry_out = [(recept_start[i] - read[i][SPAN:]).astype(bf16) for i in each]
        last = [start[i] == start_last[i] for i in each]
        moved = [nn(jnp.where(last[i], solved[i], 0.0), erase_down[i]) for i in each]
        put = [nn(jnp.where(last[i], v[i], 0.0), mixed_down[i]) for i in each]
        push = [(put[i] - moved[i][:SPAN]) * fade[i] for i in each]
        trans = [(moved[i][SPAN:] * fade[i]).astype(bf16) for i in each]
        whole = []
        for i in each:
            carried = now.astype(bf16)
            whole.append(nn(carried, carry_out[i]) + local_out[i])
            now = now * keep[i] - nn(carried, trans[i]) + push[i]
        for i in each:
            center = whole[i] - jnp.mean(whole[i], axis=0, keepdims=True)
            power2 = jnp.mean(center * center, axis=0, keepdims=True)
            line = (center * lax.rsqrt(power2 + group_eps) * scale + shift).astype(bf16)
            normed[ids[i]] = line

            @pl.when(ctx == ids[i])
            def _(i=i, line=line):
                heads[ids[i]] = line

            @pl.when(ctx != ids[i])
            def _(i=i):
                head_copy(ids[i]).start()

    rest_heads = heads.at[pl.ds(0, n_ctx - 1)]
    pltpu.make_async_copy(rest_heads, rest_heads, head_recv).wait()
    lines = jnp.concatenate(
        [heads[2 * c : 2 * c + 2].reshape(2 * SPAN, block).T for c in range(n_ctx // 2)], axis=1
    )

    def toward(n, far):
        step = n_tensor - 1 if (n % 2 == 0) != far else 1
        return lax.rem(tensor + step, n_tensor)

    def copy_to(n, kind, src, dst, other):
        return pltpu.make_async_remote_copy(
            src_ref=src,
            dst_ref=dst,
            send_sem=part_send.at[n, kind],
            recv_sem=part_recv.at[n, kind],
            device_id=(dp, ctx, other),
            device_id_type=MESH,
        )

    def raw_copy(n):
        opposite = lax.rem(tensor + 2, n_tensor)
        return copy_to(n, 0, parts.at[n, opposite], relay_in.at[n], toward(n, False))

    def straight_copy(n):
        other = toward(n, True)
        return copy_to(n, 1, parts.at[n, other], landed.at[n, 0], other)

    def sum_copy(n):
        return copy_to(n, 2, relay_out.at[n], landed.at[n, 1], toward(n, False))

    def relay(n):
        raw_copy(n).wait_recv()
        both = relay_in[n].astype(f32) + parts[n, toward(n, False)].astype(f32)
        relay_out[n] = both.astype(bf16)
        sum_copy(n).start()

    own_rows = parts.shape[2]
    for n in range(PARTS):
        weight_load(n).wait()
        product = jnp.dot(lines, weight[n], preferred_element_type=f32).astype(bf16)
        for q in range(n_tensor):
            parts[n, q] = product[q * own_rows : (q + 1) * own_rows]
        raw_copy(n).start()
        straight_copy(n).start()
        if n >= LAG:
            relay(n - LAG)
    for n in range(PARTS - LAG, PARTS):
        relay(n)
    for n in range(PARTS):
        straight_copy(n).wait_recv()
        sum_copy(n).wait_recv()
        total = parts[n, tensor].astype(f32) + landed[n, 0].astype(f32) + landed[n, 1].astype(f32)
        out_ref[:, n * width : (n + 1) * width] = total.astype(bf16)
    rest = meta.at[pl.ds(0, n_ctx - 1)]
    pltpu.make_async_copy(rest, rest, note_send).wait()
    for g in range(n_groups):
        rest = rows.at[g, pl.ds(0, n_peers - 1)]
        pltpu.make_async_copy(rest, rest, rows_send.at[g]).wait()
    pltpu.make_async_copy(rest_heads, rest_heads, head_send).wait()
    for n in range(PARTS):
        raw_copy(n).wait_send()
        straight_copy(n).wait_send()
        sum_copy(n).wait_send()


def hbm():
    return pl.BlockSpec(memory_space=pltpu.HBM)


def local(
    acceptance_vectors,
    lookup_vectors,
    payload_vectors,
    incontext_adaptation,
    fading_codes,
    stacked_line_pointer,
    article_extents,
    feature_fading,
    erasure_lookup_scaling,
    lookup_mixture_share,
    reward_coefficients,
    cluster_standard_scaling,
    cluster_standard_offset,
    final_projection,
):
    tokens, features = acceptance_vectors.shape
    columns = final_projection.shape[1]
    n_dp = lax.axis_size("dp")
    n_ctx = lax.axis_size("context")
    n_tensor = lax.axis_size("tensor")
    n_peers = n_dp * n_ctx
    n_groups = n_ctx // GROUP
    own_rows = tokens // n_tensor
    width = columns // PARTS
    vectors = [
        item.reshape(features // 128, 128)
        for item in (
            feature_fading,
            erasure_lookup_scaling,
            lookup_mixture_share,
            reward_coefficients,
            cluster_standard_scaling,
            cluster_standard_offset,
        )
    ]
    dma = pltpu.SemaphoreType.DMA
    vm = pltpu.VMEM
    summed = pl.pallas_call(
        functools.partial(layer, n_dp, n_ctx, n_tensor),
        out_shape=jax.ShapeDtypeStruct((own_rows, columns), bf16),
        in_specs=[hbm()] * 14,
        out_specs=pl.BlockSpec(memory_space=pltpu.VMEM),
        scratch_shapes=[
            vm((tokens, features), bf16),
            vm((tokens, features), bf16),
            vm((tokens, features), bf16),
            vm((tokens, features), bf16),
            vm((n_ctx, tokens), jnp.int32),
            vm((1, tokens), jnp.int32),
            vm((1, article_extents.shape[1]), jnp.int32),
            vm((6, features // 128, 128), f32),
            vm((PARTS, features, width), bf16),
            vm((n_groups, n_peers, 16, 2 * SPAN), bf16),
            vm((n_groups, n_peers, 16, 2 * SPAN), bf16),
            vm((n_peers * 16, 2 * SPAN), f32),
            vm((n_ctx, 8, tokens), f32),
            vm((n_ctx, 8, tokens), f32),
            vm((n_ctx, 4, SPAN, tokens), f32),
            vm((n_ctx, 8, tokens), f32),
            vm((n_ctx, tokens, tokens), bf16),
            vm((n_ctx, SPAN, tokens), bf16),
            vm((n_ctx, SPAN, tokens), bf16),
            vm((PARTS, n_tensor, own_rows, width), bf16),
            vm((PARTS, own_rows, width), bf16),
            vm((PARTS, own_rows, width), bf16),
            vm((PARTS, 2, own_rows, width), bf16),
            dma((13,)),
            dma((PARTS,)),
            dma((n_groups + 1,)),
            dma,
            dma,
            dma((n_groups,)),
            dma((n_groups,)),
            dma,
            dma,
            dma((PARTS, 3)),
            dma((PARTS, 3)),
        ],
        compiler_params=pltpu.CompilerParams(
            collective_id=0, has_side_effects=True, vmem_limit_bytes=60 << 20
        ),
    )(
        acceptance_vectors,
        lookup_vectors,
        payload_vectors,
        incontext_adaptation,
        fading_codes[0].T,
        stacked_line_pointer,
        article_extents,
        *vectors,
        final_projection,
    )
    return summed.reshape(1, own_rows, columns)


def solution(mesh):
    return jax.shard_map(
        local,
        mesh=mesh,
        in_specs=(
            P(("dp", "context"), "tensor"),
            P(("dp", "context"), "tensor"),
            P(("dp", "context"), "tensor"),
            P(("dp", "context"), "tensor"),
            P("dp", "context", "tensor"),
            P("dp", "context"),
            P("dp", None),
            P("tensor"),
            P("tensor"),
            P("tensor"),
            P("tensor"),
            P("tensor"),
            P("tensor"),
            P("tensor", None),
        ),
        out_specs=P("dp", ("context", "tensor"), None),
        check_vma=False,
    )
```

```python
import functools

import jax
import jax.numpy as jnp
from jax import lax
from jax.experimental import pallas as pl
from jax.experimental.pallas import tpu as pltpu
from jax.sharding import PartitionSpec as P

MESH = pl.DeviceIdType.MESH
SPAN = 64
GROUP = 4
SMALL = 8
PARTS = 8
LAG = 6
decay_cap = 0.606531
unit_eps = 1e-06
group_eps = 0.00064
f32 = jnp.float32
bf16 = jnp.bfloat16


def nn(a, b):
    return lax.dot_general(
        a.astype(bf16), b.astype(bf16), (((1,), (0,)), ((), ())), preferred_element_type=f32
    )


def layer(
    n_dp,
    n_ctx,
    n_tensor,
    r_hbm,
    k_hbm,
    v_hbm,
    a_hbm,
    code_hbm,
    ptr_hbm,
    lens_hbm,
    rate_hbm,
    gain_hbm,
    mix_hbm,
    bonus_hbm,
    scale_hbm,
    shift_hbm,
    weight_hbm,
    out_ref,
    r_ref,
    k_ref,
    v_ref,
    a_ref,
    code_ref,
    ptr_ref,
    lens_ref,
    lines_ref,
    weight,
    packed,
    rows,
    wide,
    notes,
    meta,
    pre,
    tips,
    picks,
    normed,
    heads,
    parts,
    relay_in,
    relay_out,
    landed,
    load_sem,
    weight_sem,
    own_sem,
    note_send,
    note_recv,
    rows_send,
    rows_recv,
    head_send,
    head_recv,
    part_send,
    part_recv,
):
    dp = lax.axis_index("dp")
    ctx = lax.axis_index("context")
    tensor = lax.axis_index("tensor")
    n_peers = n_dp * n_ctx
    me = dp * n_ctx + ctx
    block = r_ref.shape[0]
    n_groups = n_ctx // GROUP
    width = weight.shape[2]

    def place(index):
        return (index // n_ctx, lax.rem(index, n_ctx), tensor)

    barrier = pltpu.get_barrier_semaphore()

    def greet(step, carry):
        other = lax.rem(me + step, n_peers)
        pl.semaphore_signal(barrier, inc=1, device_id=place(other), device_id_type=MESH)
        return carry

    lax.fori_loop(1, n_peers, greet, 0)
    for step in range(1, n_tensor):
        other = lax.rem(tensor + step, n_tensor)
        pl.semaphore_signal(barrier, inc=1, device_id=(dp, ctx, other), device_id_type=MESH)

    loads = [
        (r_hbm, r_ref),
        (k_hbm, k_ref),
        (v_hbm, v_ref),
        (a_hbm, a_ref),
        (code_hbm, code_ref),
        (ptr_hbm, ptr_ref),
        (lens_hbm, lens_ref),
    ]
    for i, ref in enumerate((rate_hbm, gain_hbm, mix_hbm, bonus_hbm, scale_hbm, shift_hbm)):
        loads.append((ref, lines_ref.at[i]))
    loads = [
        pltpu.make_async_copy(src, dst, load_sem.at[i]) for i, (src, dst) in enumerate(loads)
    ]
    for load in loads:
        load.start()

    def weight_load(n):
        return pltpu.make_async_copy(
            weight_hbm.at[:, pl.ds(n * width, width)], weight.at[n], weight_sem.at[n]
        )

    for load in loads:
        load.wait()
    for n in range(PARTS):
        weight_load(n).start()

    per_seq = block // n_dp
    for pair in range(n_ctx // 2):
        lanes = slice(128 * pair, 128 * pair + 128)
        r, k, v, a = r_ref[:, lanes], k_ref[:, lanes], v_ref[:, lanes], a_ref[:, lanes]
        for half, part in ((0, slice(0, SPAN)), (1, slice(SPAN, 128))):
            rk = jnp.concatenate([r[:, part], k[:, part]], axis=1).astype(f32)
            va = jnp.concatenate([v[:, part], a[:, part]], axis=1).astype(f32)
            for s in range(n_dp):
                slot = s * n_ctx + 2 * pair + half
                for g in range(n_groups):
                    piece = slice(s * per_seq + 8 * g, s * per_seq + 8 * g + 8)
                    packed[g, slot] = jnp.concatenate([rk[piece], va[piece]], axis=0).astype(bf16)
    codes = code_ref[...].astype(f32)
    pointers = ptr_ref[...].astype(f32)
    for c in range(n_ctx):
        notes[c] = jnp.concatenate([pointers, codes[c : c + 1, :]], axis=0)

    pl.semaphore_wait(barrier, n_peers - 1 + n_tensor - 1)

    own = [pltpu.make_async_copy(notes.at[ctx], meta.at[ctx], own_sem.at[n_groups])]
    for g in range(n_groups):
        own.append(pltpu.make_async_copy(packed.at[g, me], rows.at[g, me], own_sem.at[g]))
    for copy in own:
        copy.start()

    def send_note(step, carry):
        other = lax.rem(ctx + step, n_ctx)
        pltpu.make_async_remote_copy(
            src_ref=notes.at[other],
            dst_ref=meta.at[ctx],
            send_sem=note_send,
            recv_sem=note_recv,
            device_id=(dp, other, tensor),
            device_id_type=MESH,
        ).start()
        return carry

    lax.fori_loop(1, n_ctx, send_note, 0)
    for g in range(n_groups):

        def send_rows(step, carry, g=g):
            other = lax.rem(me + step, n_peers)
            pltpu.make_async_remote_copy(
                src_ref=packed.at[g, other],
                dst_ref=rows.at[g, me],
                send_sem=rows_send.at[g],
                recv_sem=rows_recv.at[g],
                device_id=place(other),
                device_id_type=MESH,
            ).start()
            return carry

        lax.fori_loop(1, n_peers, send_rows, 0)

    odd = lax.rem(ctx, 2) == 1
    lane = lax.broadcasted_iota(jnp.int32, (block, block), 1)
    row = lax.broadcasted_iota(jnp.int32, (block, block), 0)
    flip = (lane[:SPAN] & (SPAN - 1)) == row[:SPAN]

    def column(index):
        line = lines_ref[index, pl.ds(ctx // 2, 1), :]
        line = jnp.where(odd, line[:, SPAN:], line[:, :SPAN])
        line = jnp.broadcast_to(line, (SPAN, SPAN))
        return jnp.sum(jnp.where(flip[:, :SPAN], line, 0.0), axis=1, keepdims=True) + jnp.zeros(
            (SPAN, block), f32
        )

    rate, gain, mix, bonus, scale, shift = [column(index) for index in range(6)]
    lens = lens_ref[...]
    first = lens[:, 0:1]
    second = first + lens[:, 1:2]
    third = second + lens[:, 2:3]

    def doc_start(position):
        found = jnp.where(position >= first, first, 0)
        found = jnp.where(position >= second, second, found)
        return jnp.where(position >= third, third, found)

    mid = block // 2
    sums = jnp.concatenate(
        [
            (row <= lane).astype(f32) - (row < mid).astype(f32),
            (row >= mid).astype(f32),
            (row < mid).astype(f32),
        ],
        axis=1,
    ).astype(bf16)
    eye = (row == lane).astype(f32)
    nbits = {}
    size = SMALL
    while size <= block:
        nbits[size] = (row // size) == (lane // size)
        size *= 2
    own[0].wait()
    rest = meta.at[pl.ds(0, n_ctx - 1)]
    pltpu.make_async_copy(rest, rest, note_recv).wait()
    each = range(GROUP)
    for group in range(n_groups):
        ids = [group * GROUP + b for b in each]
        decay = [-decay_cap * (1.0 - jnp.exp(-rate * meta[c, 1:2, :])) for c in ids]
        cums = []
        for d in decay:
            d0 = d.astype(bf16)
            left = d - d0.astype(f32)
            d1 = left.astype(bf16)
            d2 = (left - d1.astype(f32)).astype(bf16)
            total = nn(jnp.concatenate([d0, d1, d2], axis=0), sums)
            cums.append(total[:SPAN] + total[SPAN : 2 * SPAN] + total[2 * SPAN :])
        for i, c in enumerate(ids):
            position = c * block + lane[0:1]
            start = doc_start(position)
            about = cums[i][:, :block]
            to_end = cums[i][:, block : 2 * block]
            to_mid = cums[i][:, 2 * block :]
            pre[c, 0] = jnp.exp(about)
            pre[c, 1] = jnp.exp(-about)
            pre[c, 2] = jnp.exp(about - decay[i])
            pre[c, 3] = jnp.where(start < c * block, jnp.exp(to_mid), 0.0)
            choice = jnp.where(lane[:SPAN] < SPAN, to_end, to_end + to_mid)
            ends = jnp.exp(jnp.sum(jnp.where(flip, choice, 0.0), axis=0, keepdims=True))
            through = doc_start(c * block + block - 1 + jnp.zeros((1, block), jnp.int32)) < c * block
            ends = jnp.where(through | (lane[0:1] < SPAN), ends, 0.0)
            tips[c] = jnp.broadcast_to(ends, (8, block))
            pointer = meta[c, 0:1, :].astype(jnp.int32)
            where = (pointer & 1) * n_peers + (pointer // block)
            picks[c] = (row == where).astype(bf16)

    def head_copy(c):
        return pltpu.make_async_remote_copy(
            src_ref=normed.at[c],
            dst_ref=heads.at[ctx],
            send_sem=head_send,
            recv_sem=head_recv,
            device_id=(dp, c, tensor),
            device_id_type=MESH,
        )

    now = jnp.zeros((SPAN, SPAN), f32)
    for group in range(n_groups):
        ids = [group * GROUP + b for b in each]
        own[1 + group].wait()
        rest = rows.at[group, pl.ds(0, n_peers - 1)]
        pltpu.make_async_copy(rest, rest, rows_recv.at[group]).wait()
        wide[...] = rows[group].reshape(n_peers * 16, 2 * SPAN).astype(f32)
        got = []
        for c in ids:
            kinds = []
            for offset in (2 * (c % GROUP), 2 * (c % GROUP) + 8):
                even = wide[pl.ds(offset, n_peers, stride=16), :]
                uneven = wide[pl.ds(offset + 1, n_peers, stride=16), :]
                kinds.append(jnp.concatenate([even, uneven], axis=0).T)
            got.append(nn(jnp.concatenate(kinds, axis=0), picks[c]))
        r = [g[:SPAN] for g in got]
        k = [g[SPAN : 2 * SPAN] for g in got]
        v = [g[2 * SPAN : 3 * SPAN] for g in got]
        a = [g[3 * SPAN :] for g in got]
        position = [c * block + lane[0:1] for c in ids]
        start = [doc_start(p) for p in position]
        zeros = jnp.zeros((1, block), jnp.int32)
        start_last = [doc_start(c * block + block - 1 + zeros) for c in ids]
        scaled = [x * gain for x in k]
        unit = [
            x * lax.rsqrt(jnp.sum(x * x, axis=0, keepdims=True) + unit_eps) for x in scaled
        ]
        mixed = [k[i] * (1.0 + (a[i] - 1.0) * mix) for i in each]
        erase = [jnp.where(start[i] == position[i], 0.0, unit[i] * a[i]) for i in each]
        extra = [
            jnp.sum(r[i] * mixed[i] * (bonus + 1.0), axis=0, keepdims=True) * v[i] for i in each
        ]
        recept_up = [r[i] * pre[ids[i], 0] for i in each]
        down = [pre[c, 1] for c in ids]
        unit_up = [unit[i] * pre[ids[i], 2] for i in each]
        opening = [pre[c, 3] for c in ids]
        unit_start = [unit_up[i] * opening[i] for i in each]
        recept_start = [recept_up[i] * opening[i] for i in each]
        erase_down = [(erase[i] * down[i]).T.astype(bf16) for i in each]
        mixed_down = [(mixed[i] * down[i]).T.astype(bf16) for i in each]
        fade = [tips[c, 0:1, :SPAN] for c in ids]
        keep = [tips[c, 0:1, SPAN:] for c in ids]
        scores = [
            nn(
                jnp.concatenate([erase_down[i], mixed_down[i]], axis=0),
                jnp.concatenate([unit_up[i], recept_up[i]], axis=1),
            )
            for i in each
        ]
        inside = [row >= start[i] - ids[i] * block for i in each]
        strict = [inside[i] & (row < lane) for i in each]
        inclusive = [inside[i] & (row <= lane) for i in each]
        erase_mat = [jnp.where(strict[i], scores[i][:block, :block], 0.0) for i in each]
        read_erase = [
            jnp.where(inclusive[i], scores[i][:block, block:], 0.0).astype(bf16) for i in each
        ]
        write_mat = [
            jnp.where(strict[i], scores[i][block:, :block], 0.0).astype(bf16) for i in each
        ]
        read_write = [
            jnp.where(strict[i], scores[i][block:, block:], 0.0).astype(bf16) for i in each
        ]
        power = [jnp.where(nbits[SMALL], -x, 0.0) for x in erase_mat]
        inverse = [eye + x for x in power]
        size = 2
        while size < SMALL:
            power = [nn(x, x) for x in power]
            inverse = [inverse[i] + nn(inverse[i], power[i]) for i in each]
            size *= 2
        size = SMALL
        while size < block:
            ring = nbits[2 * size] & ~nbits[size]
            inner = [nn(jnp.where(ring, erase_mat[i], 0.0), inverse[i]) for i in each]
            inverse = [inverse[i] - nn(inverse[i], inner[i]) for i in each]
            size *= 2
        both = [
            nn(v[i], jnp.concatenate([write_mat[i], read_write[i]], axis=1)) for i in each
        ]
        solved = [
            nn(jnp.concatenate([both[i][:, :block], unit_start[i]], axis=0), inverse[i])
            for i in each
        ]
        read = [nn(solved[i], read_erase[i]) for i in each]
        local_out = [both[i][:, block:] - read[i][:SPAN] + extra[i] for i in each]
        carry_out = [(recept_start[i] - read[i][SPAN:]).astype(bf16) for i in each]
        last = [start[i] == start_last[i] for i in each]
        moved = [nn(jnp.where(last[i], solved[i], 0.0), erase_down[i]) for i in each]
        put = [nn(jnp.where(last[i], v[i], 0.0), mixed_down[i]) for i in each]
        push = [(put[i] - moved[i][:SPAN]) * fade[i] for i in each]
        trans = [(moved[i][SPAN:] * fade[i]).astype(bf16) for i in each]
        whole = []
        for i in each:
            carried = now.astype(bf16)
            whole.append(nn(carried, carry_out[i]) + local_out[i])
            now = now * keep[i] - nn(carried, trans[i]) + push[i]
        for i in each:
            center = whole[i] - jnp.mean(whole[i], axis=0, keepdims=True)
            power2 = jnp.mean(center * center, axis=0, keepdims=True)
            line = (center * lax.rsqrt(power2 + group_eps) * scale + shift).astype(bf16)
            normed[ids[i]] = line

            @pl.when(ctx == ids[i])
            def _(i=i, line=line):
                heads[ids[i]] = line

            @pl.when(ctx != ids[i])
            def _(i=i):
                head_copy(ids[i]).start()

    rest_heads = heads.at[pl.ds(0, n_ctx - 1)]
    pltpu.make_async_copy(rest_heads, rest_heads, head_recv).wait()
    lines = jnp.concatenate(
        [heads[2 * c : 2 * c + 2].reshape(2 * SPAN, block).T for c in range(n_ctx // 2)], axis=1
    )

    def toward(n, far):
        step = n_tensor - 1 if (n % 2 == 0) != far else 1
        return lax.rem(tensor + step, n_tensor)

    def copy_to(n, kind, src, dst, other):
        return pltpu.make_async_remote_copy(
            src_ref=src,
            dst_ref=dst,
            send_sem=part_send.at[n, kind],
            recv_sem=part_recv.at[n, kind],
            device_id=(dp, ctx, other),
            device_id_type=MESH,
        )

    def raw_copy(n):
        opposite = lax.rem(tensor + 2, n_tensor)
        return copy_to(n, 0, parts.at[n, opposite], relay_in.at[n], toward(n, False))

    def straight_copy(n):
        other = toward(n, True)
        return copy_to(n, 1, parts.at[n, other], landed.at[n, 0], other)

    def sum_copy(n):
        return copy_to(n, 2, relay_out.at[n], landed.at[n, 1], toward(n, False))

    def relay(n):
        raw_copy(n).wait_recv()
        both = relay_in[n].astype(f32) + parts[n, toward(n, False)].astype(f32)
        relay_out[n] = both.astype(bf16)
        sum_copy(n).start()

    own_rows = parts.shape[2]
    for n in range(PARTS):
        weight_load(n).wait()
        product = jnp.dot(lines, weight[n], preferred_element_type=f32).astype(bf16)
        for q in range(n_tensor):
            parts[n, q] = product[q * own_rows : (q + 1) * own_rows]
        raw_copy(n).start()
        straight_copy(n).start()
        if n >= LAG:
            relay(n - LAG)
    for n in range(PARTS - LAG, PARTS):
        relay(n)
    for n in range(PARTS):
        straight_copy(n).wait_recv()
        sum_copy(n).wait_recv()
        total = parts[n, tensor].astype(f32) + landed[n, 0].astype(f32) + landed[n, 1].astype(f32)
        out_ref[:, n * width : (n + 1) * width] = total.astype(bf16)
    rest = meta.at[pl.ds(0, n_ctx - 1)]
    pltpu.make_async_copy(rest, rest, note_send).wait()
    for g in range(n_groups):
        rest = rows.at[g, pl.ds(0, n_peers - 1)]
        pltpu.make_async_copy(rest, rest, rows_send.at[g]).wait()
    pltpu.make_async_copy(rest_heads, rest_heads, head_send).wait()
    for n in range(PARTS):
        raw_copy(n).wait_send()
        straight_copy(n).wait_send()
        sum_copy(n).wait_send()


def hbm():
    return pl.BlockSpec(memory_space=pltpu.HBM)


def local(
    acceptance_vectors,
    lookup_vectors,
    payload_vectors,
    incontext_adaptation,
    fading_codes,
    stacked_line_pointer,
    article_extents,
    feature_fading,
    erasure_lookup_scaling,
    lookup_mixture_share,
    reward_coefficients,
    cluster_standard_scaling,
    cluster_standard_offset,
    final_projection,
):
    tokens, features = acceptance_vectors.shape
    columns = final_projection.shape[1]
    n_dp = lax.axis_size("dp")
    n_ctx = lax.axis_size("context")
    n_tensor = lax.axis_size("tensor")
    n_peers = n_dp * n_ctx
    n_groups = n_ctx // GROUP
    own_rows = tokens // n_tensor
    width = columns // PARTS
    vectors = [
        item.reshape(features // 128, 128)
        for item in (
            feature_fading,
            erasure_lookup_scaling,
            lookup_mixture_share,
            reward_coefficients,
            cluster_standard_scaling,
            cluster_standard_offset,
        )
    ]
    dma = pltpu.SemaphoreType.DMA
    vm = pltpu.VMEM
    summed = pl.pallas_call(
        functools.partial(layer, n_dp, n_ctx, n_tensor),
        out_shape=jax.ShapeDtypeStruct((own_rows, columns), bf16),
        in_specs=[hbm()] * 14,
        out_specs=pl.BlockSpec(memory_space=pltpu.VMEM),
        scratch_shapes=[
            vm((tokens, features), bf16),
            vm((tokens, features), bf16),
            vm((tokens, features), bf16),
            vm((tokens, features), bf16),
            vm((n_ctx, tokens), jnp.int32),
            vm((1, tokens), jnp.int32),
            vm((1, article_extents.shape[1]), jnp.int32),
            vm((6, features // 128, 128), f32),
            vm((PARTS, features, width), bf16),
            vm((n_groups, n_peers, 16, 2 * SPAN), bf16),
            vm((n_groups, n_peers, 16, 2 * SPAN), bf16),
            vm((n_peers * 16, 2 * SPAN), f32),
            vm((n_ctx, 2, tokens), f32),
            vm((n_ctx, 2, tokens), f32),
            vm((n_ctx, 4, SPAN, tokens), f32),
            vm((n_ctx, 8, tokens), f32),
            vm((n_ctx, tokens, tokens), bf16),
            vm((n_ctx, SPAN, tokens), bf16),
            vm((n_ctx, SPAN, tokens), bf16),
            vm((PARTS, n_tensor, own_rows, width), bf16),
            vm((PARTS, own_rows, width), bf16),
            vm((PARTS, own_rows, width), bf16),
            vm((PARTS, 2, own_rows, width), bf16),
            dma((13,)),
            dma((PARTS,)),
            dma((n_groups + 1,)),
            dma,
            dma,
            dma((n_groups,)),
            dma((n_groups,)),
            dma,
            dma,
            dma((PARTS, 3)),
            dma((PARTS, 3)),
        ],
        compiler_params=pltpu.CompilerParams(
            collective_id=0, has_side_effects=True, vmem_limit_bytes=60 << 20
        ),
    )(
        acceptance_vectors,
        lookup_vectors,
        payload_vectors,
        incontext_adaptation,
        fading_codes[0].T,
        stacked_line_pointer,
        article_extents,
        *vectors,
        final_projection,
    )
    return summed.reshape(1, own_rows, columns)


def solution(mesh):
    return jax.shard_map(
        local,
        mesh=mesh,
        in_specs=(
            P(("dp", "context"), "tensor"),
            P(("dp", "context"), "tensor"),
            P(("dp", "context"), "tensor"),
            P(("dp", "context"), "tensor"),
            P("dp", "context", "tensor"),
            P("dp", "context"),
            P("dp", None),
            P("tensor"),
            P("tensor"),
            P("tensor"),
            P("tensor"),
            P("tensor"),
            P("tensor"),
            P("tensor", None),
        ),
        out_specs=P("dp", ("context", "tensor"), None),
        check_vma=False,
    )
```

```python
import functools

import jax
import jax.numpy as jnp
from jax import lax
from jax.experimental import pallas as pl
from jax.experimental.pallas import tpu as pltpu
from jax.sharding import PartitionSpec as P

MESH = pl.DeviceIdType.MESH
SPAN = 64
GROUP = 4
SMALL = 8
PARTS = 8
LAG = 6
decay_cap = 0.606531
unit_eps = 1e-06
group_eps = 0.00064
f32 = jnp.float32
bf16 = jnp.bfloat16


def nn(a, b):
    return lax.dot_general(
        a.astype(bf16), b.astype(bf16), (((1,), (0,)), ((), ())), preferred_element_type=f32
    )


def layer(
    n_dp,
    n_ctx,
    n_tensor,
    r_hbm,
    k_hbm,
    v_hbm,
    a_hbm,
    code_hbm,
    ptr_hbm,
    lens_hbm,
    rate_hbm,
    gain_hbm,
    mix_hbm,
    bonus_hbm,
    scale_hbm,
    shift_hbm,
    weight_hbm,
    out_ref,
    r_ref,
    k_ref,
    v_ref,
    a_ref,
    code_ref,
    ptr_ref,
    lens_ref,
    lines_ref,
    weight,
    packed,
    rows,
    wide,
    notes,
    meta,
    pre,
    tips,
    picks,
    normed,
    heads,
    parts,
    relay_in,
    relay_out,
    landed,
    load_sem,
    weight_sem,
    own_sem,
    note_send,
    note_recv,
    rows_send,
    rows_recv,
    head_send,
    head_recv,
    part_send,
    part_recv,
):
    dp = lax.axis_index("dp")
    ctx = lax.axis_index("context")
    tensor = lax.axis_index("tensor")
    n_peers = n_dp * n_ctx
    me = dp * n_ctx + ctx
    block = r_ref.shape[0]
    n_groups = n_ctx // GROUP
    width = weight.shape[2]

    def place(index):
        return (index // n_ctx, lax.rem(index, n_ctx), tensor)

    barrier = pltpu.get_barrier_semaphore()

    def greet(step, carry):
        other = lax.rem(me + step, n_peers)
        pl.semaphore_signal(barrier, inc=1, device_id=place(other), device_id_type=MESH)
        return carry

    for step in range(1, n_peers):
        greet(step, 0)
    for step in range(1, n_tensor):
        other = lax.rem(tensor + step, n_tensor)
        pl.semaphore_signal(barrier, inc=1, device_id=(dp, ctx, other), device_id_type=MESH)

    loads = [
        (r_hbm, r_ref),
        (k_hbm, k_ref),
        (v_hbm, v_ref),
        (a_hbm, a_ref),
        (code_hbm, code_ref),
        (ptr_hbm, ptr_ref),
        (lens_hbm, lens_ref),
    ]
    for i, ref in enumerate((rate_hbm, gain_hbm, mix_hbm, bonus_hbm, scale_hbm, shift_hbm)):
        loads.append((ref, lines_ref.at[i]))
    loads = [
        pltpu.make_async_copy(src, dst, load_sem.at[i]) for i, (src, dst) in enumerate(loads)
    ]
    for load in loads:
        load.start()

    def weight_load(n):
        return pltpu.make_async_copy(
            weight_hbm.at[:, pl.ds(n * width, width)], weight.at[n], weight_sem.at[n]
        )

    for load in loads:
        load.wait()

    per_seq = block // n_dp
    for pair in range(n_ctx // 2):
        lanes = slice(128 * pair, 128 * pair + 128)
        r, k, v, a = r_ref[:, lanes], k_ref[:, lanes], v_ref[:, lanes], a_ref[:, lanes]
        for half, part in ((0, slice(0, SPAN)), (1, slice(SPAN, 128))):
            rk = jnp.concatenate([r[:, part], k[:, part]], axis=1).astype(f32)
            va = jnp.concatenate([v[:, part], a[:, part]], axis=1).astype(f32)
            for s in range(n_dp):
                slot = s * n_ctx + 2 * pair + half
                for g in range(n_groups):
                    piece = slice(s * per_seq + 8 * g, s * per_seq + 8 * g + 8)
                    packed[g, slot] = jnp.concatenate([rk[piece], va[piece]], axis=0).astype(bf16)
    codes = code_ref[...].astype(f32)
    pointers = ptr_ref[...].astype(f32)
    for c in range(n_ctx):
        notes[c] = jnp.concatenate([pointers, codes[c : c + 1, :]], axis=0)

    pl.semaphore_wait(barrier, n_peers - 1 + n_tensor - 1)

    own = [pltpu.make_async_copy(notes.at[ctx], meta.at[ctx], own_sem.at[n_groups])]
    for g in range(n_groups):
        own.append(pltpu.make_async_copy(packed.at[g, me], rows.at[g, me], own_sem.at[g]))
    for copy in own:
        copy.start()

    def send_note(step, carry):
        other = lax.rem(ctx + step, n_ctx)
        pltpu.make_async_remote_copy(
            src_ref=notes.at[other],
            dst_ref=meta.at[ctx],
            send_sem=note_send,
            recv_sem=note_recv,
            device_id=(dp, other, tensor),
            device_id_type=MESH,
        ).start()
        return carry

    lax.fori_loop(1, n_ctx, send_note, 0)
    for g in range(n_groups):

        def send_rows(step, carry, g=g):
            other = lax.rem(me + step, n_peers)
            pltpu.make_async_remote_copy(
                src_ref=packed.at[g, other],
                dst_ref=rows.at[g, me],
                send_sem=rows_send.at[g],
                recv_sem=rows_recv.at[g],
                device_id=place(other),
                device_id_type=MESH,
            ).start()
            return carry

        lax.fori_loop(1, n_peers, send_rows, 0)

    for n in range(PARTS):
        weight_load(n).start()

    odd = lax.rem(ctx, 2) == 1
    lane = lax.broadcasted_iota(jnp.int32, (block, block), 1)
    row = lax.broadcasted_iota(jnp.int32, (block, block), 0)
    flip = (lane[:SPAN] & (SPAN - 1)) == row[:SPAN]

    def column(index):
        line = lines_ref[index, pl.ds(ctx // 2, 1), :]
        line = jnp.where(odd, line[:, SPAN:], line[:, :SPAN])
        line = jnp.broadcast_to(line, (SPAN, SPAN))
        return jnp.sum(jnp.where(flip[:, :SPAN], line, 0.0), axis=1, keepdims=True) + jnp.zeros(
            (SPAN, block), f32
        )

    rate, gain, mix, bonus, scale, shift = [column(index) for index in range(6)]
    lens = lens_ref[...]
    first = lens[:, 0:1]
    second = first + lens[:, 1:2]
    third = second + lens[:, 2:3]

    def doc_start(position):
        found = jnp.where(position >= first, first, 0)
        found = jnp.where(position >= second, second, found)
        return jnp.where(position >= third, third, found)

    mid = block // 2
    sums = jnp.concatenate(
        [
            (row <= lane).astype(f32) - (row < mid).astype(f32),
            (row >= mid).astype(f32),
            (row < mid).astype(f32),
        ],
        axis=1,
    ).astype(bf16)
    eye = (row == lane).astype(f32)
    nbits = {}
    size = SMALL
    while size <= block:
        nbits[size] = (row // size) == (lane // size)
        size *= 2
    own[0].wait()
    rest = meta.at[pl.ds(0, n_ctx - 1)]
    pltpu.make_async_copy(rest, rest, note_recv).wait()
    each = range(GROUP)
    for group in range(n_groups):
        ids = [group * GROUP + b for b in each]
        decay = [-decay_cap * (1.0 - jnp.exp(-rate * meta[c, 1:2, :])) for c in ids]
        cums = []
        for d in decay:
            d0 = d.astype(bf16)
            left = d - d0.astype(f32)
            d1 = left.astype(bf16)
            d2 = (left - d1.astype(f32)).astype(bf16)
            total = nn(jnp.concatenate([d0, d1, d2], axis=0), sums)
            cums.append(total[:SPAN] + total[SPAN : 2 * SPAN] + total[2 * SPAN :])
        for i, c in enumerate(ids):
            position = c * block + lane[0:1]
            start = doc_start(position)
            about = cums[i][:, :block]
            to_end = cums[i][:, block : 2 * block]
            to_mid = cums[i][:, 2 * block :]
            pre[c, 0] = jnp.exp(about)
            pre[c, 1] = jnp.exp(-about)
            pre[c, 2] = jnp.exp(about - decay[i])
            pre[c, 3] = jnp.where(start < c * block, jnp.exp(to_mid), 0.0)
            choice = jnp.where(lane[:SPAN] < SPAN, to_end, to_end + to_mid)
            ends = jnp.exp(jnp.sum(jnp.where(flip, choice, 0.0), axis=0, keepdims=True))
            through = doc_start(c * block + block - 1 + jnp.zeros((1, block), jnp.int32)) < c * block
            ends = jnp.where(through | (lane[0:1] < SPAN), ends, 0.0)
            tips[c] = jnp.broadcast_to(ends, (8, block))
            pointer = meta[c, 0:1, :].astype(jnp.int32)
            where = (pointer & 1) * n_peers + (pointer // block)
            picks[c] = (row == where).astype(bf16)

    def head_copy(c):
        return pltpu.make_async_remote_copy(
            src_ref=normed.at[c],
            dst_ref=heads.at[ctx],
            send_sem=head_send,
            recv_sem=head_recv,
            device_id=(dp, c, tensor),
            device_id_type=MESH,
        )

    now = jnp.zeros((SPAN, SPAN), f32)
    for group in range(n_groups):
        ids = [group * GROUP + b for b in each]
        own[1 + group].wait()
        rest = rows.at[group, pl.ds(0, n_peers - 1)]
        pltpu.make_async_copy(rest, rest, rows_recv.at[group]).wait()
        wide[...] = rows[group].reshape(n_peers * 16, 2 * SPAN).astype(f32)
        got = []
        for c in ids:
            kinds = []
            for offset in (2 * (c % GROUP), 2 * (c % GROUP) + 8):
                even = wide[pl.ds(offset, n_peers, stride=16), :]
                uneven = wide[pl.ds(offset + 1, n_peers, stride=16), :]
                kinds.append(jnp.concatenate([even, uneven], axis=0).T)
            got.append(nn(jnp.concatenate(kinds, axis=0), picks[c]))
        r = [g[:SPAN] for g in got]
        k = [g[SPAN : 2 * SPAN] for g in got]
        v = [g[2 * SPAN : 3 * SPAN] for g in got]
        a = [g[3 * SPAN :] for g in got]
        position = [c * block + lane[0:1] for c in ids]
        start = [doc_start(p) for p in position]
        zeros = jnp.zeros((1, block), jnp.int32)
        start_last = [doc_start(c * block + block - 1 + zeros) for c in ids]
        scaled = [x * gain for x in k]
        unit = [
            x * lax.rsqrt(jnp.sum(x * x, axis=0, keepdims=True) + unit_eps) for x in scaled
        ]
        mixed = [k[i] * (1.0 + (a[i] - 1.0) * mix) for i in each]
        erase = [jnp.where(start[i] == position[i], 0.0, unit[i] * a[i]) for i in each]
        extra = [
            jnp.sum(r[i] * mixed[i] * (bonus + 1.0), axis=0, keepdims=True) * v[i] for i in each
        ]
        recept_up = [r[i] * pre[ids[i], 0] for i in each]
        down = [pre[c, 1] for c in ids]
        unit_up = [unit[i] * pre[ids[i], 2] for i in each]
        opening = [pre[c, 3] for c in ids]
        unit_start = [unit_up[i] * opening[i] for i in each]
        recept_start = [recept_up[i] * opening[i] for i in each]
        erase_down = [(erase[i] * down[i]).T.astype(bf16) for i in each]
        mixed_down = [(mixed[i] * down[i]).T.astype(bf16) for i in each]
        fade = [tips[c, 0:1, :SPAN] for c in ids]
        keep = [tips[c, 0:1, SPAN:] for c in ids]
        scores = [
            nn(
                jnp.concatenate([erase_down[i], mixed_down[i]], axis=0),
                jnp.concatenate([unit_up[i], recept_up[i]], axis=1),
            )
            for i in each
        ]
        inside = [row >= start[i] - ids[i] * block for i in each]
        strict = [inside[i] & (row < lane) for i in each]
        inclusive = [inside[i] & (row <= lane) for i in each]
        erase_mat = [jnp.where(strict[i], scores[i][:block, :block], 0.0) for i in each]
        read_erase = [
            jnp.where(inclusive[i], scores[i][:block, block:], 0.0).astype(bf16) for i in each
        ]
        write_mat = [
            jnp.where(strict[i], scores[i][block:, :block], 0.0).astype(bf16) for i in each
        ]
        read_write = [
            jnp.where(strict[i], scores[i][block:, block:], 0.0).astype(bf16) for i in each
        ]
        power = [jnp.where(nbits[SMALL], -x, 0.0) for x in erase_mat]
        inverse = [eye + x for x in power]
        size = 2
        while size < SMALL:
            power = [nn(x, x) for x in power]
            inverse = [inverse[i] + nn(inverse[i], power[i]) for i in each]
            size *= 2
        size = SMALL
        while size < block:
            ring = nbits[2 * size] & ~nbits[size]
            inner = [nn(jnp.where(ring, erase_mat[i], 0.0), inverse[i]) for i in each]
            inverse = [inverse[i] - nn(inverse[i], inner[i]) for i in each]
            size *= 2
        both = [
            nn(v[i], jnp.concatenate([write_mat[i], read_write[i]], axis=1)) for i in each
        ]
        solved = [
            nn(jnp.concatenate([both[i][:, :block], unit_start[i]], axis=0), inverse[i])
            for i in each
        ]
        read = [nn(solved[i], read_erase[i]) for i in each]
        local_out = [both[i][:, block:] - read[i][:SPAN] + extra[i] for i in each]
        carry_out = [(recept_start[i] - read[i][SPAN:]).astype(bf16) for i in each]
        last = [start[i] == start_last[i] for i in each]
        moved = [nn(jnp.where(last[i], solved[i], 0.0), erase_down[i]) for i in each]
        put = [nn(jnp.where(last[i], v[i], 0.0), mixed_down[i]) for i in each]
        push = [(put[i] - moved[i][:SPAN]) * fade[i] for i in each]
        trans = [(moved[i][SPAN:] * fade[i]).astype(bf16) for i in each]
        whole = []
        for i in each:
            carried = now.astype(bf16)
            whole.append(nn(carried, carry_out[i]) + local_out[i])
            now = now * keep[i] - nn(carried, trans[i]) + push[i]
            center = whole[i] - jnp.mean(whole[i], axis=0, keepdims=True)
            power2 = jnp.mean(center * center, axis=0, keepdims=True)
            line = (center * lax.rsqrt(power2 + group_eps) * scale + shift).astype(bf16)
            normed[ids[i]] = line

            @pl.when(ctx == ids[i])
            def _(i=i, line=line):
                heads[ids[i]] = line

            @pl.when(ctx != ids[i])
            def _(i=i):
                head_copy(ids[i]).start()

    rest_heads = heads.at[pl.ds(0, n_ctx - 1)]
    pltpu.make_async_copy(rest_heads, rest_heads, head_recv).wait()
    lines = jnp.concatenate(
        [heads[2 * c : 2 * c + 2].reshape(2 * SPAN, block).T for c in range(n_ctx // 2)], axis=1
    )

    def toward(n, far):
        step = n_tensor - 1 if (n % 2 == 0) != far else 1
        return lax.rem(tensor + step, n_tensor)

    def copy_to(n, kind, src, dst, other):
        return pltpu.make_async_remote_copy(
            src_ref=src,
            dst_ref=dst,
            send_sem=part_send.at[n, kind],
            recv_sem=part_recv.at[n, kind],
            device_id=(dp, ctx, other),
            device_id_type=MESH,
        )

    def raw_copy(n):
        opposite = lax.rem(tensor + 2, n_tensor)
        return copy_to(n, 0, parts.at[n, opposite], relay_in.at[n], toward(n, False))

    def straight_copy(n):
        other = toward(n, True)
        return copy_to(n, 1, parts.at[n, other], landed.at[n, 0], other)

    def sum_copy(n):
        return copy_to(n, 2, relay_out.at[n], landed.at[n, 1], toward(n, False))

    def relay(n):
        raw_copy(n).wait_recv()
        both = relay_in[n].astype(f32) + parts[n, toward(n, False)].astype(f32)
        relay_out[n] = both.astype(bf16)
        sum_copy(n).start()

    own_rows = parts.shape[2]
    for n in range(PARTS):
        weight_load(n).wait()
        product = jnp.dot(lines, weight[n], preferred_element_type=f32).astype(bf16)
        for q in range(n_tensor):
            parts[n, q] = product[q * own_rows : (q + 1) * own_rows]
        raw_copy(n).start()
        straight_copy(n).start()
        if n >= LAG:
            relay(n - LAG)
    for n in range(PARTS - LAG, PARTS):
        relay(n)
    for n in range(PARTS):
        straight_copy(n).wait_recv()
        sum_copy(n).wait_recv()
        total = parts[n, tensor].astype(f32) + landed[n, 0].astype(f32) + landed[n, 1].astype(f32)
        out_ref[:, n * width : (n + 1) * width] = total.astype(bf16)
    rest = meta.at[pl.ds(0, n_ctx - 1)]
    pltpu.make_async_copy(rest, rest, note_send).wait()
    for g in range(n_groups):
        rest = rows.at[g, pl.ds(0, n_peers - 1)]
        pltpu.make_async_copy(rest, rest, rows_send.at[g]).wait()
    pltpu.make_async_copy(rest_heads, rest_heads, head_send).wait()
    for n in range(PARTS):
        raw_copy(n).wait_send()
        straight_copy(n).wait_send()
        sum_copy(n).wait_send()


def hbm():
    return pl.BlockSpec(memory_space=pltpu.HBM)


def local(
    acceptance_vectors,
    lookup_vectors,
    payload_vectors,
    incontext_adaptation,
    fading_codes,
    stacked_line_pointer,
    article_extents,
    feature_fading,
    erasure_lookup_scaling,
    lookup_mixture_share,
    reward_coefficients,
    cluster_standard_scaling,
    cluster_standard_offset,
    final_projection,
):
    tokens, features = acceptance_vectors.shape
    columns = final_projection.shape[1]
    n_dp = lax.axis_size("dp")
    n_ctx = lax.axis_size("context")
    n_tensor = lax.axis_size("tensor")
    n_peers = n_dp * n_ctx
    n_groups = n_ctx // GROUP
    own_rows = tokens // n_tensor
    width = columns // PARTS
    vectors = [
        item.reshape(features // 128, 128)
        for item in (
            feature_fading,
            erasure_lookup_scaling,
            lookup_mixture_share,
            reward_coefficients,
            cluster_standard_scaling,
            cluster_standard_offset,
        )
    ]
    dma = pltpu.SemaphoreType.DMA
    vm = pltpu.VMEM
    summed = pl.pallas_call(
        functools.partial(layer, n_dp, n_ctx, n_tensor),
        out_shape=jax.ShapeDtypeStruct((own_rows, columns), bf16),
        in_specs=[hbm()] * 14,
        out_specs=pl.BlockSpec(memory_space=pltpu.VMEM),
        scratch_shapes=[
            vm((tokens, features), bf16),
            vm((tokens, features), bf16),
            vm((tokens, features), bf16),
            vm((tokens, features), bf16),
            vm((n_ctx, tokens), jnp.int32),
            vm((1, tokens), jnp.int32),
            vm((1, article_extents.shape[1]), jnp.int32),
            vm((6, features // 128, 128), f32),
            vm((PARTS, features, width), bf16),
            vm((n_groups, n_peers, 16, 2 * SPAN), bf16),
            vm((n_groups, n_peers, 16, 2 * SPAN), bf16),
            vm((n_peers * 16, 2 * SPAN), f32),
            vm((n_ctx, 2, tokens), f32),
            vm((n_ctx, 2, tokens), f32),
            vm((n_ctx, 4, SPAN, tokens), f32),
            vm((n_ctx, 8, tokens), f32),
            vm((n_ctx, tokens, tokens), bf16),
            vm((n_ctx, SPAN, tokens), bf16),
            vm((n_ctx, SPAN, tokens), bf16),
            vm((PARTS, n_tensor, own_rows, width), bf16),
            vm((PARTS, own_rows, width), bf16),
            vm((PARTS, own_rows, width), bf16),
            vm((PARTS, 2, own_rows, width), bf16),
            dma((13,)),
            dma((PARTS,)),
            dma((n_groups + 1,)),
            dma,
            dma,
            dma((n_groups,)),
            dma((n_groups,)),
            dma,
            dma,
            dma((PARTS, 3)),
            dma((PARTS, 3)),
        ],
        compiler_params=pltpu.CompilerParams(
            collective_id=0, has_side_effects=True, vmem_limit_bytes=60 << 20
        ),
    )(
        acceptance_vectors,
        lookup_vectors,
        payload_vectors,
        incontext_adaptation,
        fading_codes[0].T,
        stacked_line_pointer,
        article_extents,
        *vectors,
        final_projection,
    )
    return summed.reshape(1, own_rows, columns)


def solution(mesh):
    return jax.shard_map(
        local,
        mesh=mesh,
        in_specs=(
            P(("dp", "context"), "tensor"),
            P(("dp", "context"), "tensor"),
            P(("dp", "context"), "tensor"),
            P(("dp", "context"), "tensor"),
            P("dp", "context", "tensor"),
            P("dp", "context"),
            P("dp", None),
            P("tensor"),
            P("tensor"),
            P("tensor"),
            P("tensor"),
            P("tensor"),
            P("tensor"),
            P("tensor", None),
        ),
        out_specs=P("dp", ("context", "tensor"), None),
        check_vma=False,
    )
```
